256 devices in a mesh: vec: 4 (over x_hi, core), grid: 64 (over y, z, x_lo).
Axes of the slice: x: 4 (x_hi: 2, x_lo: 2; x = x_hi * 2 + x_lo), y: 4, z: 8, core: 2. Of those that a mesh axis runs over, the one named last changes fastest.
Arguments:
- start_block: float32 [16, 256, 192, 256], P('vec', 'grid'), may hold values from -10 to 10
- potential: float32 [256, 192, 256], P('grid'), may hold values from 0.2 to 1.5
Outputs:
- rotated: float32 [16, 256, 192, 256], P('vec', 'grid')
- rotated_image: float32 [16, 256, 192, 256], P('vec', 'grid')
- ritz_block: float32 [16, 16], replicated
The draws below stay inside these ranges and needn't reach their ends.
All inputs are finite; a program needn't handle non-finite values.
Results may differ from the reference program's by a relative error of at most 0.00014.
Values sent between devices are 32-bit elements; how exact they have to be, the bound alone decides.
A program may use at most 128 MiB of HBM per device.

```python
import jax
import jax.numpy as jnp
from jax import lax

NY = 192
NZ = 256
V = 16
NX = 256


def draw_start_block(key, part):
    key = jax.random.fold_in(key, 7)
    plane_index = jnp.arange(NX, dtype=jnp.float32).reshape(1, NX, 1, 1)
    amplitude = 0.6 + 1.2 * plane_index / jnp.float32(max(NX - 1, 1))
    noise = jax.random.normal(jax.random.fold_in(key, 1), (V, NX, NY, NZ), jnp.float32)
    values = noise * amplitude
    return jnp.clip(values, -10.0, 10.0)


def block_scale(key, shape, cuts, smallest, top_value):
    def one(position, parts):
        draws = jax.random.uniform(jax.random.fold_in(jax.random.fold_in(key, 6), position), (parts,), jnp.float32, smallest / len(cuts), top_value / len(cuts))
        return jnp.repeat(jnp.exp(draws), shape[position] // parts).reshape((-1,) + (1,) * (len(shape) - position - 1))

    gain = one(*cuts[0])
    for cut in cuts[1:]:
        gain = gain * one(*cut)
    return gain


def setup_inputs(seed: int = 0) -> dict:
    splits = jax.random.split(jax.random.key(seed), 3)
    return {
        "start_block": draw_start_block(jax.random.fold_in(splits[2], 71), 0),
        "potential": jnp.clip(0.2 + 1.3 * jax.random.uniform(splits[1], (NX, NY, NZ), jnp.float32) ** block_scale(splits[1], (NX, NY, NZ), ((0, 64),), -0.2, 0.2), 0.2, 1.5),
    }


AXIAL_COEF = 0.25
CROSS_COEF = 0.25
FILTER_MID = 3.0
FILTER_HALF = 2.0

def op_ext(padded, coef_mid):
    center_planes = padded[..., 2:-2, :, :]
    axial = AXIAL_COEF * (2.5 * center_planes - 4.0 / 3.0 * (padded[..., 1:-3, :, :] + padded[..., 3:-1, :, :]) + 1.0 / 12.0 * (padded[..., 0:-4, :, :] + padded[..., 4:, :, :]))
    pad_side = [(0, 0)] * (center_planes.ndim - 2)
    along_y = jnp.pad(center_planes, pad_side + [(1, 1), (0, 0)])
    along_z = jnp.pad(center_planes, pad_side + [(0, 0), (1, 1)])
    cross_y = CROSS_COEF * (2.0 * center_planes - along_y[..., :-2, :] - along_y[..., 2:, :])
    cross_z = CROSS_COEF * (2.0 * center_planes - along_z[..., :-2] - along_z[..., 2:])
    return axial + cross_y + cross_z + coef_mid * center_planes

def wrap_planes(field):
    return jnp.concatenate([field[..., -2:, :, :], field, field[..., :2, :, :]], axis=-3)

def reference(start_block, potential):

    def filter_one(vector):
        first_pass = (op_ext(wrap_planes(vector), potential) - FILTER_MID * vector) / FILTER_HALF
        second_pass = 2.0 * (op_ext(wrap_planes(first_pass), potential) - FILTER_MID * first_pass) / FILTER_HALF - vector
        applied = op_ext(wrap_planes(second_pass), potential)
        return (second_pass, applied)
    second_pass, applied = lax.map(filter_one, start_block)
    flat_block = second_pass.reshape(V, -1)
    flat_applied = applied.reshape(V, -1)
    dims = (((1,), (1,)), ((), ()))
    gram = lax.dot_general(flat_block.astype(jnp.float32), flat_block.astype(jnp.float32), dims, precision=lax.Precision.HIGHEST, preferred_element_type=jnp.float32)
    curvature = lax.dot_general(flat_block.astype(jnp.float32), flat_applied.astype(jnp.float32), dims, precision=lax.Precision.HIGHEST, preferred_element_type=jnp.float32)
    factor = jnp.linalg.cholesky(gram)
    inverse = jax.scipy.linalg.solve_triangular(factor, jnp.eye(V, dtype=jnp.float32), lower=True)
    ritz_block = jnp.dot(jnp.dot(inverse, curvature, precision=lax.Precision.HIGHEST), inverse.T, precision=lax.Precision.HIGHEST)
    norm_scale = jnp.sqrt(jnp.float32(NX * NY * NZ))
    rotated = jnp.dot(inverse, flat_block, precision=lax.Precision.HIGHEST) * norm_scale
    rotated_image = jnp.dot(inverse, flat_applied, precision=lax.Precision.HIGHEST) * norm_scale
    return (rotated.reshape(start_block.shape), rotated_image.reshape(start_block.shape), ritz_block)
```

```python
import functools

import jax
import jax.numpy as jnp
from jax import lax
from jax.experimental import pallas as pl
from jax.experimental.pallas import tpu as pltpu
from jax.sharding import PartitionSpec as P

MESH = pl.DeviceIdType.MESH
F32 = jnp.float32
HI = lax.Precision.HIGHEST
NX, NY, NZ = 4, 4, 8
VPG, GROUPS = 4, 4
PLANES = 4
ROWS = 48
LANES = 256
TOP, BOT = 8, 8 + ROWS
STEP = 16
NT = (((1,), (1,)), ((), ()))


def place():
    vec, grid = lax.axis_index("vec"), lax.axis_index("grid")
    return (vec // 2) * 2 + grid % 2, grid // (2 * NZ), (grid // 2) % NZ, vec % 2


def device(x, y, z, core):
    return ((x // 2) * 2 + core, (y * NZ + z) * 2 + x % 2)


def stencil(src, pot, i, g, p, row, scale, middle):
    rows = pl.ds(row, STEP)
    at = lambda q, r: src[i, g, q, pl.ds(r, STEP), :]
    center = at(p + 2, row)
    lane = lax.broadcasted_iota(jnp.int32, (STEP, LANES), 1)
    left = jnp.where(lane == 0, 0.0, pltpu.roll(center, 1, 1))
    right = jnp.where(lane == LANES - 1, 0.0, pltpu.roll(center, LANES - 1, 1))
    cross = (at(p + 2, row - 1) + at(p + 2, row + 1)) + (left + right)
    near = at(p + 1, row) + at(p + 3, row)
    far = at(p, row) + at(p + 4, row)
    diag = scale * pot[p, pl.ds(row - TOP, STEP), :] + scale * (1.625 - middle)
    return diag * center - (scale / 3.0) * near + (scale / 48.0) * far - (scale * 0.25) * cross


def kernel(start, pot, rot_out, img_out, ritz_out,
           xs, fs, ss, aa, rr, ii, pw, ysend, yrecv, gp, red, mat, inv_s,
           a_send, a_recv, p_send, p_recv, h_send, h_recv, y_send, y_recv,
           r_send, r_recv, o_send, o_recv, s_sem):
    x, y, z, c = place()
    x_lo = x % 2
    mine = lax.axis_index("vec")
    k = y * NZ + z
    ring = NY * NZ

    def at_ring(kk, core):
        kk = (kk + ring) % ring
        return device(x, kk // NZ, kk % NZ, core)

    right = at_ring(k + c, 1 - c)
    left = at_ring(k - (1 - c), 1 - c)
    line = [device(((2 * x + c + d) % 8) // 2, y, z, ((2 * x + c + d) % 8) % 2) for d in range(1, 8)]
    z_peers = [device(x, y, (z + d) % NZ, c) for d in range(1, NZ)]
    y_peers = [device(x, (y + d) % NY, z, c) for d in range(1, NY)]
    far = at_ring(k + 2 * c - 1, 1 - c)

    barrier = pltpu.get_barrier_semaphore()
    peers = line + z_peers + y_peers + [far]
    for peer in peers:
        pl.semaphore_signal(barrier, inc=1, device_id=peer, device_id_type=MESH)
    pl.semaphore_wait(barrier, len(peers))

    def remote(src, dst, send, recv, to):
        return pltpu.make_async_remote_copy(
            src_ref=src, dst_ref=dst, send_sem=send, recv_sem=recv, device_id=to, device_id_type=MESH)

    own_rows = pl.ds(TOP, ROWS)

    def pot_local():
        return pltpu.make_async_copy(pot.at[:, pl.ds(pl.multiple_of(ROWS * x, 8), ROWS), :], pw, p_recv)

    pair_x = x + 1 - 2 * x_lo
    pot_remote = remote(pot.at[:, pl.ds(pl.multiple_of(ROWS * pair_x, 8), ROWS), :], pw, p_send, p_recv,
                        device(pair_x, y, z, c))

    @pl.when(c == x_lo)
    def _():
        pot_local().start()
        pot_remote.start()

    def a_copy(i, d):
        to = (x + d) % NX
        src = start.at[i, :, pl.ds(pl.multiple_of(ROWS * to, 8), ROWS), :]
        dst = xs.at[i, mine, 2:2 + PLANES, own_rows, :]
        return src, dst, to

    def a_remote(i, d):
        src, dst, to = a_copy(i, d)
        return remote(src, dst, a_send.at[i, d], a_recv.at[i, mine], device(to, y, z, x_lo))

    @pl.loop(0, VPG)
    def _(i):
        for d in (2, 1, 3):
            a_remote(i, d).start()

        @pl.when(c == x_lo)
        def _():
            src, dst, _ = a_copy(i, 0)
            pltpu.make_async_copy(src, dst, a_recv.at[i, mine]).start()

        @pl.when(c != x_lo)
        def _():
            a_remote(i, 0).start()

    def a_wait(i):
        for g in range(GROUPS):
            dst = xs.at[i, g, 2:2 + PLANES, own_rows, :]
            remote(dst, dst, a_send.at[i, 0], a_recv.at[i, g], right).wait_recv()

    top_keep = jnp.where(x == 0, 0.0, 1.0).astype(F32)
    bot_keep = jnp.where(x == NX - 1, 0.0, 1.0).astype(F32)
    above = device((x + NX - 1) % NX, y, z, c)
    below = device((x + 1) % NX, y, z, c)

    def halo_copies(buf, s, i):
        return (
            remote(buf.at[i, :, PLANES:PLANES + 2, own_rows, :], buf.at[i, :, 0:2, own_rows, :],
                   h_send.at[s, i, 0], h_recv.at[s, i, 0], right),
            remote(buf.at[i, :, 2:4, own_rows, :], buf.at[i, :, PLANES + 2:PLANES + 4, own_rows, :],
                   h_send.at[s, i, 1], h_recv.at[s, i, 1], left),
            remote(ysend.at[s, i, 0], yrecv.at[s, i, 0], y_send.at[s, i, 0], y_recv.at[s, i, 0], below),
            remote(ysend.at[s, i, 1], yrecv.at[s, i, 1], y_send.at[s, i, 1], y_recv.at[s, i, 1], above),
        )

    def halo_start(buf, s, i):
        @pl.loop(0, GROUPS)
        def _(g):
            for p in range(PLANES):
                ysend[s, i, 0, g, pl.ds(p, 1), :] = buf[i, g, p + 2, pl.ds(BOT - 1, 1), :]
                ysend[s, i, 1, g, pl.ds(p, 1), :] = buf[i, g, p + 2, pl.ds(TOP, 1), :]

        for copy in halo_copies(buf, s, i):
            copy.start()

    def halo_wait(buf, s, i):
        for copy in halo_copies(buf, s, i):
            copy.wait_recv()

        @pl.loop(0, GROUPS)
        def _(g):
            for p in range(PLANES):
                buf[i, g, p + 2, pl.ds(TOP - 1, 1), :] = yrecv[s, i, 0, g, pl.ds(p, 1), :] * top_keep
                buf[i, g, p + 2, pl.ds(BOT, 1), :] = yrecv[s, i, 1, g, pl.ds(p, 1), :] * bot_keep

    def first(i):
        halo_wait(xs, 0, i)

        @pl.loop(0, GROUPS)
        def _(g):
            for p in range(PLANES):
                for row in range(TOP, BOT, STEP):
                    fs[i, g, p + 2, pl.ds(row, STEP), :] = stencil(xs, pw, i, g, p, row, 0.5, 3.0)

        halo_start(fs, 1, i)

    def blocks(i, other, off):
        @pl.loop(0, i + 1)
        def _(j):
            def body(t, accs):
                p, r = t // (ROWS // 8), t % (ROWS // 8)
                row = pl.multiple_of(TOP + 8 * r, 8)
                a = [ss[i, g, p + 2, pl.ds(row, 8), :] for g in range(GROUPS)]
                if off:
                    b = [other[j, h, p, pl.ds(pl.multiple_of(8 * r, 8), 8), :] for h in range(GROUPS)]
                else:
                    b = [other[j, h, p + 2, pl.ds(row, 8), :] for h in range(GROUPS)]
                new = []
                for g in range(GROUPS):
                    for h in range(GROUPS):
                        prod = a[g] * b[h]
                        new.append(accs[g * GROUPS + h] + (prod[:, :128] + prod[:, 128:]))
                return tuple(new)

            zero = jnp.zeros((8, 128), F32)
            accs = lax.fori_loop(0, PLANES * ROWS // 8, body, (zero,) * (GROUPS * GROUPS))
            for g in range(GROUPS):
                for h in range(GROUPS):
                    gp[g * VPG + i, h * VPG + j] = accs[g * GROUPS + h]

            @pl.when(j < i)
            def _():
                for g in range(GROUPS):
                    for h in range(GROUPS):
                        gp[h * VPG + j, g * VPG + i] = accs[g * GROUPS + h]

    def second(i):
        halo_wait(fs, 1, i)

        @pl.loop(0, GROUPS)
        def _(g):
            for p in range(PLANES):
                for row in range(TOP, BOT, STEP):
                    rows = pl.ds(row, STEP)
                    ss[i, g, p + 2, rows, :] = (
                        stencil(fs, pw, i, g, p, row, 1.0, 3.0) - xs[i, g, p + 2, rows, :])

        halo_start(ss, 2, i)
        blocks(i, ss, False)

    def image(i):
        halo_wait(ss, 2, i)

        @pl.loop(0, GROUPS)
        def _(g):
            for p in range(PLANES):
                for row in range(TOP, BOT, STEP):
                    aa[i, g, p, pl.ds(row - TOP, STEP), :] = stencil(ss, pw, i, g, p, row, 1.0, 0.0)

    line_slot = 2 * x + c
    lane16 = lax.broadcasted_iota(jnp.int32, (16, 128), 1)

    def gather_tiles():
        def body(u, out):
            tile = jnp.sum(gp[u], axis=1)
            return jnp.where(lane16 == u, jnp.sum(tile, axis=1, keepdims=True), out)

        return lax.fori_loop(0, 16, body, jnp.zeros((16, 128), F32))

    rounds = ((line, 0, 8, line_slot), (z_peers, 8, NZ, z), (y_peers, 8 + NZ, NY, y))

    def round_copies(w, n):
        to, base, count, own = rounds[n]
        slot = base + own
        return [remote(red.at[w, slot], red.at[w, slot], r_send.at[w, base + d], r_recv.at[w, slot], peer)
                for d, peer in enumerate(to)]

    def round_start(w, n, value):
        to, base, count, own = rounds[n]
        red[w, base + own] = value
        for copy in round_copies(w, n):
            copy.start()

    def round_sum(w, n):
        to, base, count, own = rounds[n]
        for d, peer in enumerate(to):
            slot = base + (own + d + 1) % count
            remote(red.at[w, slot], red.at[w, slot], r_send.at[w, base + d], r_recv.at[w, slot], peer).wait_recv()
        total = red[w, base]
        for q in range(1, count):
            total = total + red[w, base + q]
        return total

    pot_wait = remote(pw, pw, p_send, p_recv, right)

    @pl.loop(0, VPG + 1)
    def _(t):
        @pl.when(t < VPG)
        def _():
            a_wait(t)
            halo_start(xs, 0, t)

        @pl.when(t == 0)
        def _():
            pot_wait.wait_recv()

        @pl.when(t > 0)
        def _():
            second(t - 1)

        @pl.when(t < VPG)
        def _():
            first(t)

    round_start(0, 0, gather_tiles())
    image(0)
    round_start(0, 1, round_sum(0, 0))
    image(1)
    round_start(0, 2, round_sum(0, 1))
    image(2)
    gram = round_sum(0, 2)

    row16 = lax.broadcasted_iota(jnp.int32, (16, 128), 0)
    work = jnp.where(lane16 < 16, gram, jnp.where(lane16 - 16 == row16, 1.0, 0.0))
    for j in range(16):
        scale = 1.0 / jnp.sqrt(work[j:j + 1, j:j + 1])
        pivot = work[j:j + 1, :] * scale
        column = work[:, j:j + 1] * scale
        work = jnp.where(row16 > j, work - column * pivot, jnp.where(row16 == j, pivot, work))
    inverse = jnp.where(lane16 < 16, pltpu.roll(work, 112, 1), 0.0)
    norm = jnp.sqrt(jnp.full((16, 128), PLANES * 64 * ROWS * NX * LANES, F32))
    mat[...] = inverse * norm
    to_smem = pltpu.make_async_copy(mat, inv_s, s_sem)
    to_smem.start()
    to_smem.wait()

    def o_copy(out, buf, w, i, g):
        to_x = 2 * (g // 2) + c
        to_c = g % 2
        dst = out.at[i, :, pl.ds(pl.multiple_of(ROWS * x, 8), ROWS), :]
        here = jnp.logical_and(to_x == x, to_c == c)
        send = remote(buf.at[i, g], dst, o_send.at[w, i, g], o_recv.at[w, i, x], device(to_x, y, z, to_c))
        keep = pltpu.make_async_copy(buf.at[i, g], dst, o_recv.at[w, i, x])
        return here, send, keep

    def rotate(src, lift, buf, out, w):
        @pl.loop(0, VPG * GROUPS)
        def _(n):
            i, g = n // GROUPS, n % GROUPS
            v = g * VPG + i
            coef = [inv_s[v, u] for u in range(16)]

            @pl.loop(0, PLANES)
            def _(p):
                for row in range(0, ROWS, STEP):
                    acc = None
                    for u in range(16):
                        term = coef[u] * src[u % VPG, u // VPG, p + lift, pl.ds(row + (TOP if lift else 0), STEP), :]
                        acc = term if acc is None else acc + term
                    buf[i, g, p, pl.ds(row, STEP), :] = acc

            here, send, keep = o_copy(out, buf, w, i, g)

            @pl.when(here)
            def _():
                keep.start()

            @pl.when(jnp.logical_not(here))
            def _():
                send.start()

    rotate(ss, 2, rr, rot_out, 0)
    image(3)
    rotate(aa, 0, ii, img_out, 1)

    @pl.loop(0, VPG)
    def _(i):
        blocks(i, aa, True)

    round_start(1, 0, gather_tiles())
    round_start(1, 1, round_sum(1, 0))
    round_start(1, 2, round_sum(1, 1))
    curvature = round_sum(1, 2)
    half = lax.dot_general(inverse, curvature, NT, precision=HI, preferred_element_type=F32)
    half = jnp.concatenate([half, jnp.zeros((16, 112), F32)], axis=1)
    ritz_out[...] = lax.dot_general(half, inverse, NT, precision=HI, preferred_element_type=F32)

    @pl.when(c == x_lo)
    def _():
        pot_remote.wait_send()

    @pl.loop(0, VPG)
    def _(i):
        for d in (1, 2, 3):
            a_remote(i, d).wait_send()

        @pl.when(c != x_lo)
        def _():
            a_remote(i, 0).wait_send()

        for s, buf in enumerate((xs, fs, ss)):
            for copy in halo_copies(buf, s, i):
                copy.wait_send()

    for w in range(2):
        for n in range(3):
            for copy in round_copies(w, n):
                copy.wait_send()

    for w, (out, buf) in enumerate(((rot_out, rr), (img_out, ii))):
        @pl.loop(0, VPG * GROUPS)
        def _(n):
            i, g = n // GROUPS, n % GROUPS
            here, send, keep = o_copy(out, buf, w, i, g)

            @pl.when(jnp.logical_not(here))
            def _():
                send.wait_send()

        @pl.loop(0, VPG)
        def _(i):
            for xx in range(NX):
                dst = out.at[i, :, pl.ds(ROWS * xx, ROWS), :]
                remote(dst, dst, o_send.at[w, i, 0], o_recv.at[w, i, xx], right).wait_recv()


def body(start_block, potential):
    dma = pltpu.SemaphoreType.DMA
    any_space = pl.BlockSpec(memory_space=pl.ANY)
    field = pltpu.VMEM((VPG, GROUPS, PLANES + 4, ROWS + 16, LANES), F32)
    inner = pltpu.VMEM((VPG, GROUPS, PLANES, ROWS, LANES), F32)
    return tuple(pl.pallas_call(
        kernel,
        out_shape=(
            jax.ShapeDtypeStruct(start_block.shape, F32),
            jax.ShapeDtypeStruct(start_block.shape, F32),
            jax.ShapeDtypeStruct((16, 16), F32),
        ),
        in_specs=[any_space, any_space],
        out_specs=(any_space, any_space, pl.BlockSpec(memory_space=pltpu.VMEM)),
        scratch_shapes=[
            field, field, field, inner, inner, inner,
            pltpu.VMEM((PLANES, ROWS, LANES), F32),
            pltpu.VMEM((3, VPG, 2, GROUPS, PLANES, LANES), F32),
            pltpu.VMEM((3, VPG, 2, GROUPS, PLANES, LANES), F32),
            pltpu.VMEM((16, 16, 8, 128), F32),
            pltpu.VMEM((2, 8 + NZ + NY, 16, 128), F32),
            pltpu.VMEM((16, 128), F32),
            pltpu.SMEM((16, 128), F32),
            dma((VPG, 4)), dma((VPG, GROUPS)), dma, dma,
            dma((3, VPG, 2)), dma((3, VPG, 2)), dma((3, VPG, 2)), dma((3, VPG, 2)),
            dma((2, 8 + NZ + NY)), dma((2, 8 + NZ + NY)),
            dma((2, VPG, GROUPS)), dma((2, VPG, NX)), dma,
        ],
        compiler_params=pltpu.CompilerParams(
            collective_id=0, has_side_effects=True, vmem_limit_bytes=56 * 2**20),
        name="filtered_subspace",
    )(start_block, potential))


def solution(mesh):
    in_specs = (P("vec", "grid", None, None), P("grid", None, None))
    out_specs = (P("vec", "grid", None, None), P("vec", "grid", None, None), P())
    return jax.shard_map(body, mesh=mesh, in_specs=in_specs, out_specs=out_specs, check_vma=False)
```

```python
import functools

import jax
import jax.numpy as jnp
from jax import lax
from jax.experimental import pallas as pl
from jax.experimental.pallas import tpu as pltpu
from jax.sharding import PartitionSpec as P

MESH = pl.DeviceIdType.MESH
F32 = jnp.float32
HI = lax.Precision.HIGHEST
NX, NY, NZ = 4, 4, 8
VPG, GROUPS = 4, 4
PLANES = 4
ROWS = 48
LANES = 256
TOP, BOT = 8, 8 + ROWS
STEP = 16
NT = (((1,), (1,)), ((), ()))


def place():
    vec, grid = lax.axis_index("vec"), lax.axis_index("grid")
    return (vec // 2) * 2 + grid % 2, grid // (2 * NZ), (grid // 2) % NZ, vec % 2


def device(x, y, z, core):
    return ((x // 2) * 2 + core, (y * NZ + z) * 2 + x % 2)


def stencil(src, pot, i, g, p, row, scale, middle):
    rows = pl.ds(row, STEP)
    at = lambda q, r: src[i, g, q, pl.ds(r, STEP), :]
    center = at(p + 2, row)
    lane = lax.broadcasted_iota(jnp.int32, (STEP, LANES), 1)
    left = jnp.where(lane == 0, 0.0, pltpu.roll(center, 1, 1))
    right = jnp.where(lane == LANES - 1, 0.0, pltpu.roll(center, LANES - 1, 1))
    cross = (at(p + 2, row - 1) + at(p + 2, row + 1)) + (left + right)
    near = at(p + 1, row) + at(p + 3, row)
    far = at(p, row) + at(p + 4, row)
    diag = scale * pot[p, pl.ds(row - TOP, STEP), :] + scale * (1.625 - middle)
    return diag * center - (scale / 3.0) * near + (scale / 48.0) * far - (scale * 0.25) * cross


def kernel(start, pot, rot_out, img_out, ritz_out,
           xs, fs, ss, aa, rr, ii, pw, edge, pack, xy, ysend, yrecv, gp, red, mat, inv_s,
           a_send, a_recv, e_sem, k_send, k_recv, p_send, p_recv, h_send, h_recv, y_send, y_recv,
           r_send, r_recv, o_send, o_recv, s_sem):
    x, y, z, c = place()
    x_lo = x % 2
    mine = lax.axis_index("vec")
    k = y * NZ + z
    ring = NY * NZ

    def at_ring(kk, core):
        kk = (kk + ring) % ring
        return device(x, kk // NZ, kk % NZ, core)

    right = at_ring(k + c, 1 - c)
    left = at_ring(k - (1 - c), 1 - c)
    line = [device(((2 * x + c + d) % 8) // 2, y, z, ((2 * x + c + d) % 8) % 2) for d in range(1, 8)]
    z_peers = [device(x, y, (z + d) % NZ, c) for d in range(1, NZ)]
    y_peers = [device(x, (y + d) % NY, z, c) for d in range(1, NY)]
    far = at_ring(k + 2 * c - 1, 1 - c)

    barrier = pltpu.get_barrier_semaphore()
    peers = line + z_peers + y_peers + [far]
    for peer in peers:
        pl.semaphore_signal(barrier, inc=1, device_id=peer, device_id_type=MESH)
    pl.semaphore_wait(barrier, len(peers))

    def remote(src, dst, send, recv, to):
        return pltpu.make_async_remote_copy(
            src_ref=src, dst_ref=dst, send_sem=send, recv_sem=recv, device_id=to, device_id_type=MESH)

    own_rows = pl.ds(TOP, ROWS)

    def pot_local():
        return pltpu.make_async_copy(pot.at[:, pl.ds(pl.multiple_of(ROWS * x, 8), ROWS), :], pw, p_recv)

    pair_x = x + 1 - 2 * x_lo
    pot_remote = remote(pot.at[:, pl.ds(pl.multiple_of(ROWS * pair_x, 8), ROWS), :], pw, p_send, p_recv,
                        device(pair_x, y, z, c))

    @pl.when(c == x_lo)
    def _():
        pot_local().start()
        pot_remote.start()

    def a_copy(i, d):
        to = (x + d) % NX
        src = start.at[i, :, pl.ds(pl.multiple_of(ROWS * to, 8), ROWS), :]
        dst = xs.at[i, mine, 2:2 + PLANES, own_rows, :]
        return src, dst, to

    def a_remote(i, d):
        src, dst, to = a_copy(i, d)
        return remote(src, dst, a_send.at[i, d], a_recv.at[i, mine], device(to, y, z, x_lo))

    def a_start(i):
        for d in (2, 1, 3):
            a_remote(i, d).start()

        @pl.when(c == x_lo)
        def _():
            src, dst, _ = a_copy(i, 0)
            pltpu.make_async_copy(src, dst, a_recv.at[i, mine]).start()

        @pl.when(c != x_lo)
        def _():
            a_remote(i, 0).start()

    def e_copy(b):
        return pltpu.make_async_copy(start.at[:, :, pl.ds(ROWS * (b + 1) - 8, 16), :], edge.at[b], e_sem.at[b])

    def k_remote(d):
        to = (x + d) % NX
        return remote(pack.at[to], xy.at[mine], k_send.at[d], k_recv.at[mine], device(to, y, z, x_lo))

    for b in range(NX - 1):
        e_copy(b).start()
    a_start(0)
    for b in range(NX - 1):
        e_copy(b).wait()

    @pl.loop(0, VPG)
    def _(i):
        for p in range(PLANES):
            for q in range(NX):
                zero = jnp.zeros((1, LANES), F32)
                above_row = edge[q - 1, i, p, pl.ds(7, 1), :] if q else zero
                below_row = edge[q, i, p, pl.ds(8, 1), :] if q < NX - 1 else zero
                pack[q, i, 0, pl.ds(p, 1), :] = above_row
                pack[q, i, 1, pl.ds(p, 1), :] = below_row

    for d in (2, 1, 3):
        k_remote(d).start()

    @pl.when(c == x_lo)
    def _():
        pltpu.make_async_copy(pack.at[x], xy.at[mine], k_recv.at[mine]).start()

    @pl.when(c != x_lo)
    def _():
        k_remote(0).start()

    @pl.loop(1, VPG)
    def _(i):
        a_start(i)

    def a_wait(n):
        i, h = n // 2, n % 2
        for e in range(2):
            dst = xs.at[i, 2 * h + e, 2:2 + PLANES, own_rows, :]
            remote(dst, dst, a_send.at[i, 0], a_recv.at[i, 2 * h + e], right).wait_recv()

    top_keep = jnp.where(x == 0, 0.0, 1.0).astype(F32)
    bot_keep = jnp.where(x == NX - 1, 0.0, 1.0).astype(F32)
    above = device((x + NX - 1) % NX, y, z, c)
    below = device((x + 1) % NX, y, z, c)

    def plane_copies(buf, s, n):
        i, gs = n // 2, pl.ds(2 * (n % 2), 2)
        return (
            remote(buf.at[i, gs, PLANES:PLANES + 2, own_rows, :], buf.at[i, gs, 0:2, own_rows, :],
                   h_send.at[s, n, 0], h_recv.at[s, n, 0], right),
            remote(buf.at[i, gs, 2:4, own_rows, :], buf.at[i, gs, PLANES + 2:PLANES + 4, own_rows, :],
                   h_send.at[s, n, 1], h_recv.at[s, n, 1], left),
        )

    def row_copies(s, n):
        return (
            remote(ysend.at[s, n, 0], yrecv.at[s, n, 0], y_send.at[s, n, 0], y_recv.at[s, n, 0], below),
            remote(ysend.at[s, n, 1], yrecv.at[s, n, 1], y_send.at[s, n, 1], y_recv.at[s, n, 1], above),
        )

    def row_start(buf, s, n):
        i, h = n // 2, n % 2
        for e in range(2):
            for p in range(PLANES):
                ysend[s, n, 0, e, pl.ds(p, 1), :] = buf[i, 2 * h + e, p + 2, pl.ds(BOT - 1, 1), :]
                ysend[s, n, 1, e, pl.ds(p, 1), :] = buf[i, 2 * h + e, p + 2, pl.ds(TOP, 1), :]

        for copy in row_copies(s, n):
            copy.start()

    def plane_start(buf, s, n):
        for copy in plane_copies(buf, s, n):
            copy.start()

    def plane_wait(buf, s, n):
        for copy in plane_copies(buf, s, n):
            copy.wait_recv()

    def row_wait(buf, s, n):
        i, h = n // 2, n % 2
        for copy in row_copies(s, n):
            copy.wait_recv()

        for e in range(2):
            for p in range(PLANES):
                buf[i, 2 * h + e, p + 2, pl.ds(TOP - 1, 1), :] = yrecv[s, n, 0, e, pl.ds(p, 1), :] * top_keep
                buf[i, 2 * h + e, p + 2, pl.ds(BOT, 1), :] = yrecv[s, n, 1, e, pl.ds(p, 1), :] * bot_keep

    def first(n):
        i = n // 2
        plane_wait(xs, 0, n)

        @pl.loop(0, 2)
        def _(e):
            g = 2 * (n % 2) + e
            for p in range(PLANES):
                xs[i, g, p + 2, pl.ds(TOP - 1, 1), :] = xy[g, i, 0, pl.ds(p, 1), :]
                xs[i, g, p + 2, pl.ds(BOT, 1), :] = xy[g, i, 1, pl.ds(p, 1), :]
            for p in range(PLANES):
                for row in range(TOP, BOT, STEP):
                    fs[i, g, p + 2, pl.ds(row, STEP), :] = stencil(xs, pw, i, g, p, row, 0.5, 3.0)

        plane_start(fs, 1, n)
        row_start(fs, 0, n)

    def block(i, gs, j, other, off):
        def step(t, accs):
            p, r = t // (ROWS // 8), t % (ROWS // 8)
            row = pl.multiple_of(TOP + 8 * r, 8)
            a = [ss[i, g, p + 2, pl.ds(row, 8), :] for g in gs]
            if off:
                b = [other[j, h, p, pl.ds(pl.multiple_of(8 * r, 8), 8), :] for h in range(GROUPS)]
            else:
                b = [other[j, h, p + 2, pl.ds(row, 8), :] for h in range(GROUPS)]
            new = []
            for q in range(len(gs)):
                for h in range(GROUPS):
                    prod = a[q] * b[h]
                    new.append(accs[q * GROUPS + h] + (prod[:, :128] + prod[:, 128:]))
            return tuple(new)

        zero = jnp.zeros((8, 128), F32)
        return lax.fori_loop(0, PLANES * ROWS // 8, step, (zero,) * (len(gs) * GROUPS))

    def blocks(n, other, off):
        i, h = n // 2, n % 2

        @pl.loop(0, i)
        def _(j):
            gs = (2 * h, 2 * h + 1)
            accs = block(i, gs, j, other, off)
            for q, g in enumerate(gs):
                for o in range(GROUPS):
                    gp[g * VPG + i, o * VPG + j] = accs[q * GROUPS + o]
                    gp[o * VPG + j, g * VPG + i] = accs[q * GROUPS + o]

        @pl.when(h == 1)
        def _():
            accs = block(i, range(GROUPS), i, other, off)
            for g in range(GROUPS):
                for o in range(GROUPS):
                    gp[g * VPG + i, o * VPG + i] = accs[g * GROUPS + o]

    def second(n):
        i = n // 2
        plane_wait(fs, 1, n)
        row_wait(fs, 0, n)

        @pl.loop(0, 2)
        def _(e):
            g = 2 * (n % 2) + e
            for p in range(PLANES):
                for row in range(TOP, BOT, STEP):
                    rows = pl.ds(row, STEP)
                    ss[i, g, p + 2, rows, :] = (
                        stencil(fs, pw, i, g, p, row, 1.0, 3.0) - xs[i, g, p + 2, rows, :])

        blocks(n, ss, False)

    def image(n):
        i = n // 2
        plane_wait(ss, 2, n)
        row_wait(ss, 1, n)

        @pl.loop(0, 2)
        def _(e):
            g = 2 * (n % 2) + e
            for p in range(PLANES):
                for row in range(TOP, BOT, STEP):
                    aa[i, g, p, pl.ds(row - TOP, STEP), :] = stencil(ss, pw, i, g, p, row, 1.0, 0.0)

        blocks(n, aa, True)

    line_slot = 2 * x + c
    lane16 = lax.broadcasted_iota(jnp.int32, (16, 128), 1)

    def gather_tiles():
        out = jnp.zeros((16, 128), F32)
        for u in range(16):
            tile = jnp.sum(gp[u], axis=1)
            out = jnp.where(lane16 == u, jnp.sum(tile, axis=1, keepdims=True), out)
        return out

    rounds = ((line, 0, 8, line_slot), (z_peers, 8, NZ, z), (y_peers, 8 + NZ, NY, y))

    def round_copies(w, n):
        to, base, count, own = rounds[n]
        slot = base + own
        return [remote(red.at[w, slot], red.at[w, slot], r_send.at[w, base + d], r_recv.at[w, slot], peer)
                for d, peer in enumerate(to)]

    def round_start(w, n, value):
        to, base, count, own = rounds[n]
        red[w, base + own] = value
        for copy in round_copies(w, n):
            copy.start()

    def round_sum(w, n):
        to, base, count, own = rounds[n]
        for d, peer in enumerate(to):
            slot = base + (own + d + 1) % count
            remote(red.at[w, slot], red.at[w, slot], r_send.at[w, base + d], r_recv.at[w, slot], peer).wait_recv()
        total = red[w, base]
        for q in range(1, count):
            total = total + red[w, base + q]
        return total

    pot_wait = remote(pw, pw, p_send, p_recv, right)

    parts = 2 * VPG

    @pl.loop(0, VPG)
    def _(i):
        for h in range(2):
            a_wait(2 * i + h)
            plane_start(xs, 0, 2 * i + h)

        @pl.when(i == 0)
        def _():
            pot_wait.wait_recv()
            for g in range(GROUPS):
                remote(xy.at[g], xy.at[g], k_send.at[0], k_recv.at[g], right).wait_recv()

        @pl.when(i < VPG - 1)
        def _():
            @pl.loop(0, 2)
            def _(h):
                first(2 * i + h)

    @pl.loop(0, parts)
    def _(t):
        @pl.when(jnp.logical_and(t >= parts - 4, t < parts - 2))
        def _():
            first(t + 2)

        second(t)

    round_start(0, 0, gather_tiles())
    round_start(0, 1, round_sum(0, 0))
    round_start(0, 2, round_sum(0, 1))

    gram = round_sum(0, 2)

    row16 = lax.broadcasted_iota(jnp.int32, (16, 128), 0)
    work = jnp.where(lane16 < 16, gram, jnp.where(lane16 - 16 == row16, 1.0, 0.0))
    for j in range(15):
        column = work[:, j:j + 1] * (1.0 / work[j:j + 1, j:j + 1])
        work = work - jnp.where(row16 > j, column, 0.0) * work[j:j + 1, :]
    pivots = jnp.sum(jnp.where(lane16 == row16, work, 0.0), axis=1, keepdims=True)
    work = work * (1.0 / jnp.sqrt(pivots))
    inverse = jnp.where(lane16 < 16, pltpu.roll(work, 112, 1), 0.0)
    norm = jnp.sqrt(jnp.full((16, 128), PLANES * 64 * ROWS * NX * LANES, F32))
    mat[...] = inverse * norm
    to_smem = pltpu.make_async_copy(mat, inv_s, s_sem)
    to_smem.start()
    to_smem.wait()

    def o_copy(out, buf, w, i, g):
        to_x = 2 * (g // 2) + c
        to_c = g % 2
        dst = out.at[i, :, pl.ds(pl.multiple_of(ROWS * x, 8), ROWS), :]
        here = jnp.logical_and(to_x == x, to_c == c)
        send = remote(buf.at[i, g], dst, o_send.at[w, i, g], o_recv.at[w, i, x], device(to_x, y, z, to_c))
        keep = pltpu.make_async_copy(buf.at[i, g], dst, o_recv.at[w, i, x])
        return here, send, keep

    def rotate(src, lift, buf, out, w, begin, end):
        @pl.loop(begin * GROUPS, end * GROUPS)
        def _(n):
            i, g = n // GROUPS, n % GROUPS
            v = g * VPG + i
            coef = [inv_s[v, u] for u in range(16)]

            @pl.loop(0, PLANES)
            def _(p):
                for row in range(0, ROWS, STEP):
                    acc = None
                    for u in range(16):
                        term = coef[u] * src[u % VPG, u // VPG, p + lift, pl.ds(row + (TOP if lift else 0), STEP), :]
                        acc = term if acc is None else acc + term
                    buf[i, g, p, pl.ds(row, STEP), :] = acc

            here, send, keep = o_copy(out, buf, w, i, g)

            @pl.when(here)
            def _():
                keep.start()

            @pl.when(jnp.logical_not(here))
            def _():
                send.start()

    @pl.loop(0, parts)
    def _(t):
        plane_start(ss, 2, t)
        row_start(ss, 1, t)

    rotate(ss, 2, rr, rot_out, 0, 0, VPG)

    @pl.loop(0, parts)
    def _(t):
        image(t)

    round_start(1, 1, gather_tiles())
    rotate(aa, 0, ii, img_out, 1, 0, 1)
    round_start(1, 2, round_sum(1, 1))
    rotate(aa, 0, ii, img_out, 1, 1, 2)
    round_start(1, 0, round_sum(1, 2))
    rotate(aa, 0, ii, img_out, 1, 2, VPG)
    curvature = round_sum(1, 0)
    half = lax.dot_general(inverse, curvature, NT, precision=HI, preferred_element_type=F32)
    half = jnp.concatenate([half, jnp.zeros((16, 112), F32)], axis=1)
    ritz_out[...] = lax.dot_general(half, inverse, NT, precision=HI, preferred_element_type=F32)

    @pl.when(c == x_lo)
    def _():
        pot_remote.wait_send()

    @pl.loop(0, VPG)
    def _(i):
        for d in (1, 2, 3):
            a_remote(i, d).wait_send()

        @pl.when(c != x_lo)
        def _():
            a_remote(i, 0).wait_send()

    @pl.loop(0, parts)
    def _(t):
        for s, buf in enumerate((xs, fs, ss)):
            for copy in plane_copies(buf, s, t):
                copy.wait_send()
        for s in range(2):
            for copy in row_copies(s, t):
                copy.wait_send()

    for d in (1, 2, 3):
        k_remote(d).wait_send()

    @pl.when(c != x_lo)
    def _():
        k_remote(0).wait_send()

    for w in range(2):
        for n in range(3):
            for copy in round_copies(w, n):
                copy.wait_send()

    for w, (out, buf) in enumerate(((rot_out, rr), (img_out, ii))):
        @pl.loop(0, VPG * GROUPS)
        def _(n):
            i, g = n // GROUPS, n % GROUPS
            here, send, keep = o_copy(out, buf, w, i, g)

            @pl.when(jnp.logical_not(here))
            def _():
                send.wait_send()

        @pl.loop(0, VPG)
        def _(i):
            for xx in range(NX):
                dst = out.at[i, :, pl.ds(ROWS * xx, ROWS), :]
                remote(dst, dst, o_send.at[w, i, 0], o_recv.at[w, i, xx], right).wait_recv()


def body(start_block, potential):
    dma = pltpu.SemaphoreType.DMA
    any_space = pl.BlockSpec(memory_space=pl.ANY)
    field = pltpu.VMEM((VPG, GROUPS, PLANES + 4, ROWS + 16, LANES), F32)
    inner = pltpu.VMEM((VPG, GROUPS, PLANES, ROWS, LANES), F32)
    return tuple(pl.pallas_call(
        kernel,
        out_shape=(
            pltpu.VMEM(start_block.shape, F32),
            pltpu.VMEM(start_block.shape, F32),
            jax.ShapeDtypeStruct((16, 16), F32),
        ),
        in_specs=[any_space, any_space],
        out_specs=(pl.BlockSpec(memory_space=pltpu.VMEM), pl.BlockSpec(memory_space=pltpu.VMEM), pl.BlockSpec(memory_space=pltpu.VMEM)),
        scratch_shapes=[
            field, field, field, inner, inner, inner,
            pltpu.VMEM((PLANES, ROWS, LANES), F32),
            pltpu.VMEM((NX - 1, VPG, PLANES, 16, LANES), F32),
            pltpu.VMEM((NX, VPG, 2, PLANES, LANES), F32),
            pltpu.VMEM((GROUPS, VPG, 2, PLANES, LANES), F32),
            pltpu.VMEM((2, 2 * VPG, 2, 2, PLANES, LANES), F32),
            pltpu.VMEM((2, 2 * VPG, 2, 2, PLANES, LANES), F32),
            pltpu.VMEM((16, 16, 8, 128), F32),
            pltpu.VMEM((2, 8 + NZ + NY, 16, 128), F32),
            pltpu.VMEM((16, 128), F32),
            pltpu.SMEM((16, 128), F32),
            dma((VPG, 4)), dma((VPG, GROUPS)), dma((NX - 1,)), dma((NX,)), dma((GROUPS,)), dma, dma,
            dma((3, 2 * VPG, 2)), dma((3, 2 * VPG, 2)), dma((2, 2 * VPG, 2)), dma((2, 2 * VPG, 2)),
            dma((2, 8 + NZ + NY)), dma((2, 8 + NZ + NY)),
            dma((2, VPG, GROUPS)), dma((2, VPG, NX)), dma,
        ],
        compiler_params=pltpu.CompilerParams(
            collective_id=0, has_side_effects=True, vmem_limit_bytes=48 * 2**20),
        name="filtered_subspace",
    )(start_block, potential))


def solution(mesh):
    in_specs = (P("vec", "grid", None, None), P("grid", None, None))
    out_specs = (P("vec", "grid", None, None), P("vec", "grid", None, None), P())
    return jax.shard_map(body, mesh=mesh, in_specs=in_specs, out_specs=out_specs, check_vma=False)
```

```python
import functools

import jax
import jax.numpy as jnp
from jax import lax
from jax.experimental import pallas as pl
from jax.experimental.pallas import tpu as pltpu
from jax.sharding import PartitionSpec as P

MESH = pl.DeviceIdType.MESH
F32 = jnp.float32
HI = lax.Precision.HIGHEST
NX, NY, NZ = 4, 4, 8
VPG, GROUPS = 4, 4
PLANES = 4
ROWS = 48
LANES = 256
TOP, BOT = 8, 8 + ROWS
STEP = 16
AHEAD = 2
NT = (((1,), (1,)), ((), ()))


def place():
    vec, grid = lax.axis_index("vec"), lax.axis_index("grid")
    return (vec // 2) * 2 + grid % 2, grid // (2 * NZ), (grid // 2) % NZ, vec % 2


def device(x, y, z, core):
    return ((x // 2) * 2 + core, (y * NZ + z) * 2 + x % 2)


def stencil(src, pot, i, g, p, row, scale, middle):
    rows = pl.ds(row, STEP)
    at = lambda q, r: src[i, g, q, pl.ds(r, STEP), :]
    center = at(p + 2, row)
    lane = lax.broadcasted_iota(jnp.int32, (STEP, LANES), 1)
    left = jnp.where(lane == 0, 0.0, pltpu.roll(center, 1, 1))
    right = jnp.where(lane == LANES - 1, 0.0, pltpu.roll(center, LANES - 1, 1))
    cross = (at(p + 2, row - 1) + at(p + 2, row + 1)) + (left + right)
    near = at(p + 1, row) + at(p + 3, row)
    far = at(p, row) + at(p + 4, row)
    diag = scale * pot[p, pl.ds(row - TOP, STEP), :] + scale * (1.625 - middle)
    return diag * center - (scale / 3.0) * near + (scale / 48.0) * far - (scale * 0.25) * cross


def kernel(start, pot, rot_out, img_out, ritz_out,
           xs, fs, ss, aa, rr, ii, pw, edge, pack, xy, ysend, yrecv, gp, red, mat, ps, sib, inv_s,
           a_send, a_recv, e_sem, k_send, k_recv, p_send, p_recv, h_send, h_recv, y_send, y_recv,
           r_send, r_recv, o_send, o_recv, q_send, q_recv, t_send, t_recv, s_sem):
    x, y, z, c = place()
    x_lo = x % 2
    mine = lax.axis_index("vec")
    k = y * NZ + z
    ring = NY * NZ

    def at_ring(kk, core):
        kk = (kk + ring) % ring
        return device(x, kk // NZ, kk % NZ, core)

    right = at_ring(k + c, 1 - c)
    left = at_ring(k - (1 - c), 1 - c)
    line = [device(((2 * x + c + d) % 8) // 2, y, z, ((2 * x + c + d) % 8) % 2) for d in range(1, 8)]
    z_peers = [device(x, y, (z + d) % NZ, c) for d in range(1, NZ)]
    y_peers = [device(x, (y + d) % NY, z, c) for d in range(1, NY)]
    far = at_ring(k + 2 * c - 1, 1 - c)

    barrier = pltpu.get_barrier_semaphore()
    peers = line + z_peers + y_peers + [far]
    for peer in peers:
        pl.semaphore_signal(barrier, inc=1, device_id=peer, device_id_type=MESH)
    pl.semaphore_wait(barrier, len(peers))

    def remote(src, dst, send, recv, to):
        return pltpu.make_async_remote_copy(
            src_ref=src, dst_ref=dst, send_sem=send, recv_sem=recv, device_id=to, device_id_type=MESH)

    own_rows = pl.ds(TOP, ROWS)

    def pot_local():
        return pltpu.make_async_copy(pot.at[:, pl.ds(pl.multiple_of(ROWS * x, 8), ROWS), :], pw, p_recv)

    pair_x = x + 1 - 2 * x_lo
    pot_remote = remote(pot.at[:, pl.ds(pl.multiple_of(ROWS * pair_x, 8), ROWS), :], pw, p_send, p_recv,
                        device(pair_x, y, z, c))

    @pl.when(c == x_lo)
    def _():
        pot_local().start()
        pot_remote.start()

    def a_copy(i, d):
        to = (x + d) % NX
        src = start.at[i, :, pl.ds(pl.multiple_of(ROWS * to, 8), ROWS), :]
        dst = xs.at[i, mine, 2:2 + PLANES, own_rows, :]
        return src, dst, to

    def a_remote(i, d):
        src, dst, to = a_copy(i, d)
        return remote(src, dst, a_send.at[i, d], a_recv.at[i, mine], device(to, y, z, x_lo))

    def a_start(i):
        for d in (2, 1, 3):
            a_remote(i, d).start()

        @pl.when(c == x_lo)
        def _():
            src, dst, _ = a_copy(i, 0)
            pltpu.make_async_copy(src, dst, a_recv.at[i, mine]).start()

        @pl.when(c != x_lo)
        def _():
            a_remote(i, 0).start()

    def e_copy(b):
        return pltpu.make_async_copy(start.at[:, :, pl.ds(ROWS * (b + 1) - 8, 16), :], edge.at[b], e_sem.at[b])

    def k_remote(d):
        to = (x + d) % NX
        return remote(pack.at[to], xy.at[mine], k_send.at[d], k_recv.at[mine], device(to, y, z, x_lo))

    for b in range(NX - 1):
        e_copy(b).start()
    a_start(0)
    for b in range(NX - 1):
        e_copy(b).wait()

    @pl.loop(0, VPG)
    def _(i):
        for p in range(PLANES):
            for q in range(NX):
                zero = jnp.zeros((1, LANES), F32)
                above_row = edge[q - 1, i, p, pl.ds(7, 1), :] if q else zero
                below_row = edge[q, i, p, pl.ds(8, 1), :] if q < NX - 1 else zero
                pack[q, i, 0, pl.ds(p, 1), :] = above_row
                pack[q, i, 1, pl.ds(p, 1), :] = below_row

    for d in (2, 1, 3):
        k_remote(d).start()

    @pl.when(c == x_lo)
    def _():
        pltpu.make_async_copy(pack.at[x], xy.at[mine], k_recv.at[mine]).start()

    @pl.when(c != x_lo)
    def _():
        k_remote(0).start()

    @pl.loop(1, VPG)
    def _(i):
        a_start(i)

    def a_wait(n):
        i, h = n // 2, n % 2
        for e in range(2):
            dst = xs.at[i, 2 * h + e, 2:2 + PLANES, own_rows, :]
            remote(dst, dst, a_send.at[i, 0], a_recv.at[i, 2 * h + e], right).wait_recv()

    top_keep = jnp.where(x == 0, 0.0, 1.0).astype(F32)
    bot_keep = jnp.where(x == NX - 1, 0.0, 1.0).astype(F32)
    above = device((x + NX - 1) % NX, y, z, c)
    below = device((x + 1) % NX, y, z, c)

    def plane_copies(buf, s, n):
        i, gs = n // 2, pl.ds(2 * (n % 2), 2)
        return (
            remote(buf.at[i, gs, PLANES:PLANES + 2, own_rows, :], buf.at[i, gs, 0:2, own_rows, :],
                   h_send.at[s, n, 0], h_recv.at[s, n, 0], right),
            remote(buf.at[i, gs, 2:4, own_rows, :], buf.at[i, gs, PLANES + 2:PLANES + 4, own_rows, :],
                   h_send.at[s, n, 1], h_recv.at[s, n, 1], left),
        )

    def row_copies(s, n):
        return (
            remote(ysend.at[s, n, 0], yrecv.at[s, n, 0], y_send.at[s, n, 0], y_recv.at[s, n, 0], below),
            remote(ysend.at[s, n, 1], yrecv.at[s, n, 1], y_send.at[s, n, 1], y_recv.at[s, n, 1], above),
        )

    def row_start(buf, s, n):
        i, h = n // 2, n % 2
        for e in range(2):
            for p in range(PLANES):
                ysend[s, n, 0, e, pl.ds(p, 1), :] = buf[i, 2 * h + e, p + 2, pl.ds(BOT - 1, 1), :]
                ysend[s, n, 1, e, pl.ds(p, 1), :] = buf[i, 2 * h + e, p + 2, pl.ds(TOP, 1), :]

        for copy in row_copies(s, n):
            copy.start()

    def plane_start(buf, s, n):
        for copy in plane_copies(buf, s, n):
            copy.start()

    def plane_wait(buf, s, n):
        for copy in plane_copies(buf, s, n):
            copy.wait_recv()

    def row_wait(buf, s, n):
        i, h = n // 2, n % 2
        for copy in row_copies(s, n):
            copy.wait_recv()

        for e in range(2):
            for p in range(PLANES):
                buf[i, 2 * h + e, p + 2, pl.ds(TOP - 1, 1), :] = yrecv[s, n, 0, e, pl.ds(p, 1), :] * top_keep
                buf[i, 2 * h + e, p + 2, pl.ds(BOT, 1), :] = yrecv[s, n, 1, e, pl.ds(p, 1), :] * bot_keep

    def first(n):
        i = n // 2
        plane_wait(xs, 0, n)

        @pl.loop(0, 2)
        def _(e):
            g = 2 * (n % 2) + e
            for p in range(PLANES):
                xs[i, g, p + 2, pl.ds(TOP - 1, 1), :] = xy[g, i, 0, pl.ds(p, 1), :]
                xs[i, g, p + 2, pl.ds(BOT, 1), :] = xy[g, i, 1, pl.ds(p, 1), :]
            for p in range(PLANES):
                for row in range(TOP, BOT, STEP):
                    fs[i, g, p + 2, pl.ds(row, STEP), :] = stencil(xs, pw, i, g, p, row, 0.5, 3.0)

        plane_start(fs, 1, n)
        row_start(fs, 0, n)

    def block(i, gs, j, other, off):
        def step(t, accs):
            p, r = t // (ROWS // 8), t % (ROWS // 8)
            row = pl.multiple_of(TOP + 8 * r, 8)
            a = [ss[i, g, p + 2, pl.ds(row, 8), :] for g in gs]
            if off:
                b = [other[j, h, p, pl.ds(pl.multiple_of(8 * r, 8), 8), :] for h in range(GROUPS)]
            else:
                b = [other[j, h, p + 2, pl.ds(row, 8), :] for h in range(GROUPS)]
            new = []
            for q in range(len(gs)):
                for h in range(GROUPS):
                    prod = a[q] * b[h]
                    new.append(accs[q * GROUPS + h] + (prod[:, :128] + prod[:, 128:]))
            return tuple(new)

        zero = jnp.zeros((8, 128), F32)
        return lax.fori_loop(0, PLANES * ROWS // 8, step, (zero,) * (len(gs) * GROUPS))

    def blocks(n, other, off):
        i, h = n // 2, n % 2

        @pl.loop(0, i)
        def _(j):
            gs = (2 * h, 2 * h + 1)
            accs = block(i, gs, j, other, off)
            for q, g in enumerate(gs):
                for o in range(GROUPS):
                    gp[g * VPG + i, o * VPG + j] = accs[q * GROUPS + o]
                    gp[o * VPG + j, g * VPG + i] = accs[q * GROUPS + o]

        @pl.when(h == 1)
        def _():
            accs = block(i, range(GROUPS), i, other, off)
            for g in range(GROUPS):
                for o in range(GROUPS):
                    gp[g * VPG + i, o * VPG + i] = accs[g * GROUPS + o]

    def q_copy(i, j):
        to_x, to_c = 2 * (j // 2) + c, j % 2
        src = ss.at[i, :, 2 + PLANES - AHEAD + to_c, own_rows, :]
        dst = ps.at[i, :, pl.ds(pl.multiple_of(ROWS * x, 8), ROWS), :]
        here = jnp.logical_and(to_x == x, to_c == c)
        send = remote(src, dst, q_send.at[i, j], q_recv.at[i, x], device(to_x, y, z, to_c))
        return here, send, pltpu.make_async_copy(src, dst, q_recv.at[i, x])

    def q_start(i):
        for j in range(4):
            here, send, keep = q_copy(i, j)

            @pl.when(here)
            def _():
                keep.start()

            @pl.when(jnp.logical_not(here))
            def _():
                send.start()

    def second(n):
        i = n // 2
        plane_wait(fs, 1, n)
        row_wait(fs, 0, n)

        @pl.when(n == 2 * VPG - 1)
        def _():
            @pl.loop(0, VPG)
            def _(t):
                plane_start(ss, 2, t)

        @pl.loop(0, 2)
        def _(e):
            g = 2 * (n % 2) + e
            for p in range(PLANES):
                for row in range(TOP, BOT, STEP):
                    rows = pl.ds(row, STEP)
                    ss[i, g, p + 2, rows, :] = (
                        stencil(fs, pw, i, g, p, row, 1.0, 3.0) - xs[i, g, p + 2, rows, :])

        row_start(ss, 1, n)
        blocks(n, ss, False)

    def image(n):
        i = n // 2
        plane_wait(ss, 2, n)
        row_wait(ss, 1, n)

        @pl.loop(0, 2)
        def _(e):
            g = 2 * (n % 2) + e
            for p in range(PLANES):
                for row in range(TOP, BOT, STEP):
                    aa[i, g, p, pl.ds(row - TOP, STEP), :] = stencil(ss, pw, i, g, p, row, 1.0, 0.0)

        blocks(n, aa, True)

    line_slot = 2 * x + c
    lane16 = lax.broadcasted_iota(jnp.int32, (16, 128), 1)

    def gather_tiles():
        out = jnp.zeros((16, 128), F32)
        for u in range(16):
            tile = jnp.sum(gp[u], axis=1)
            out = jnp.where(lane16 == u, jnp.sum(tile, axis=1, keepdims=True), out)
        return out

    rounds = ((line, 0, 8, line_slot), (z_peers, 8, NZ, z), (y_peers, 8 + NZ, NY, y))

    def round_copies(w, n):
        to, base, count, own = rounds[n]
        slot = base + own
        return [remote(red.at[w, slot], red.at[w, slot], r_send.at[w, base + d], r_recv.at[w, slot], peer)
                for d, peer in enumerate(to)]

    def round_start(w, n, value):
        to, base, count, own = rounds[n]
        red[w, base + own] = value
        for copy in round_copies(w, n):
            copy.start()

    def round_sum(w, n):
        to, base, count, own = rounds[n]
        for d, peer in enumerate(to):
            slot = base + (own + d + 1) % count
            remote(red.at[w, slot], red.at[w, slot], r_send.at[w, base + d], r_recv.at[w, slot], peer).wait_recv()
        total = red[w, base]
        for q in range(1, count):
            total = total + red[w, base + q]
        return total

    pot_wait = remote(pw, pw, p_send, p_recv, right)

    parts = 2 * VPG

    @pl.loop(0, VPG)
    def _(i):
        for h in range(2):
            a_wait(2 * i + h)
            plane_start(xs, 0, 2 * i + h)

        @pl.when(i == 0)
        def _():
            pot_wait.wait_recv()
            for g in range(GROUPS):
                remote(xy.at[g], xy.at[g], k_send.at[0], k_recv.at[g], right).wait_recv()

        @pl.when(i < VPG - 1)
        def _():
            @pl.loop(0, 2)
            def _(h):
                first(2 * i + h)

    @pl.loop(0, parts)
    def _(t):
        @pl.when(jnp.logical_and(t >= parts - 4, t < parts - 2))
        def _():
            first(t + 2)

        second(t)

        @pl.when(t == 1)
        def _():
            q_start(0)

        @pl.when(t == parts - 3)
        def _():
            q_start(1)

    round_start(0, 0, gather_tiles())
    q_start(2)
    q_start(3)
    round_start(0, 1, round_sum(0, 0))
    round_start(0, 2, round_sum(0, 1))

    gram = round_sum(0, 2)

    row16 = lax.broadcasted_iota(jnp.int32, (16, 128), 0)
    work = jnp.where(lane16 < 16, gram, jnp.where(lane16 - 16 == row16, 1.0, 0.0))
    for j in range(15):
        column = work[:, j:j + 1] * (1.0 / work[j:j + 1, j:j + 1])
        work = work - jnp.where(row16 > j, column, 0.0) * work[j:j + 1, :]
    pivots = jnp.sum(jnp.where(lane16 == row16, work, 0.0), axis=1, keepdims=True)
    work = work * (1.0 / jnp.sqrt(pivots))
    inverse = jnp.where(lane16 < 16, pltpu.roll(work, 112, 1), 0.0)
    norm = jnp.sqrt(jnp.full((16, 128), PLANES * 64 * ROWS * NX * LANES, F32))
    mat[...] = inverse * norm
    to_smem = pltpu.make_async_copy(mat, inv_s, s_sem)
    to_smem.start()
    to_smem.wait()

    sent = (PLANES - AHEAD, PLANES)

    def o_copy(out, buf, w, i, g):
        to_x = 2 * (g // 2) + c
        to_c = g % 2
        src = buf.at[i, g, 0:sent[w]]
        dst = out.at[i, 0:sent[w], pl.ds(pl.multiple_of(ROWS * x, 8), ROWS), :]
        here = jnp.logical_and(to_x == x, to_c == c)
        send = remote(src, dst, o_send.at[w, i, g], o_recv.at[w, i, x], device(to_x, y, z, to_c))
        keep = pltpu.make_async_copy(src, dst, o_recv.at[w, i, x])
        return here, send, keep

    def rotate(src, lift, buf, out, w, begin, end):
        @pl.loop(begin * GROUPS, end * GROUPS)
        def _(n):
            i, g = n // GROUPS, n % GROUPS
            v = g * VPG + i
            coef = [inv_s[v, u] for u in range(16)]

            @pl.loop(0, sent[w])
            def _(p):
                for row in range(0, ROWS, STEP):
                    acc = None
                    for u in range(16):
                        term = coef[u] * src[u % VPG, u // VPG, p + lift, pl.ds(row + (TOP if lift else 0), STEP), :]
                        acc = term if acc is None else acc + term
                    buf[i, g, p, pl.ds(row, STEP), :] = acc

            here, send, keep = o_copy(out, buf, w, i, g)

            @pl.when(here)
            def _():
                keep.start()

            @pl.when(jnp.logical_not(here))
            def _():
                send.start()

    sibling = device(x, y, z, 1 - c)
    my_plane = PLANES - AHEAD + c

    def t_copy(i):
        return remote(sib.at[i], rot_out.at[i, my_plane], t_send.at[i], t_recv.at[i], sibling)

    def rotate_ahead(core, store):
        @pl.loop(0, VPG)
        def _(i):
            v = (2 * (x // 2) + core) * VPG + i
            coef = [inv_s[v, u] for u in range(16)]

            @pl.loop(0, NX * ROWS // STEP)
            def _(r):
                rows = pl.ds(pl.multiple_of(r * STEP, STEP), STEP)
                acc = None
                for u in range(16):
                    term = coef[u] * ps[u % VPG, u // VPG, rows, :]
                    acc = term if acc is None else acc + term
                store(i, rows, acc)

    def to_sibling(i, rows, value):
        sib[i, rows, :] = value

    def to_output(i, rows, value):
        rot_out[i, my_plane, rows, :] = value

    @pl.loop(VPG, parts)
    def _(t):
        plane_start(ss, 2, t)

    rotate(ss, 2, rr, rot_out, 0, 0, VPG)

    @pl.loop(0, VPG)
    def _(i):
        for xx in range(NX):
            dst = ps.at[i, :, pl.ds(ROWS * xx, ROWS), :]
            remote(dst, dst, q_send.at[i, 0], q_recv.at[i, xx], right).wait_recv()

    rotate_ahead(1 - c, to_sibling)

    @pl.loop(0, VPG)
    def _(i):
        t_copy(i).start()

    rotate_ahead(c, to_output)

    @pl.loop(0, parts)
    def _(t):
        image(t)

    round_start(1, 1, gather_tiles())
    rotate(aa, 0, ii, img_out, 1, 0, 1)
    round_start(1, 2, round_sum(1, 1))
    rotate(aa, 0, ii, img_out, 1, 1, 2)
    round_start(1, 0, round_sum(1, 2))
    rotate(aa, 0, ii, img_out, 1, 2, VPG)
    curvature = round_sum(1, 0)
    half = lax.dot_general(inverse, curvature, NT, precision=HI, preferred_element_type=F32)
    half = jnp.concatenate([half, jnp.zeros((16, 112), F32)], axis=1)
    ritz_out[...] = lax.dot_general(half, inverse, NT, precision=HI, preferred_element_type=F32)

    @pl.when(c == x_lo)
    def _():
        pot_remote.wait_send()

    @pl.loop(0, VPG)
    def _(i):
        for d in (1, 2, 3):
            a_remote(i, d).wait_send()

        @pl.when(c != x_lo)
        def _():
            a_remote(i, 0).wait_send()

    @pl.loop(0, parts)
    def _(t):
        for s, buf in enumerate((xs, fs, ss)):
            for copy in plane_copies(buf, s, t):
                copy.wait_send()
        for s in range(2):
            for copy in row_copies(s, t):
                copy.wait_send()

    @pl.loop(0, VPG)
    def _(i):
        t_copy(i).wait_send()
        theirs = rot_out.at[i, 2 * PLANES - 2 * AHEAD + 1 - my_plane]
        remote(theirs, theirs, t_send.at[i], t_recv.at[i], sibling).wait_recv()
        for j in range(4):
            here, send, keep = q_copy(i, j)

            @pl.when(jnp.logical_not(here))
            def _():
                send.wait_send()

    for d in (1, 2, 3):
        k_remote(d).wait_send()

    @pl.when(c != x_lo)
    def _():
        k_remote(0).wait_send()

    for w in range(2):
        for n in range(3):
            for copy in round_copies(w, n):
                copy.wait_send()

    for w, (out, buf) in enumerate(((rot_out, rr), (img_out, ii))):
        @pl.loop(0, VPG * GROUPS)
        def _(n):
            i, g = n // GROUPS, n % GROUPS
            here, send, keep = o_copy(out, buf, w, i, g)

            @pl.when(jnp.logical_not(here))
            def _():
                send.wait_send()

        @pl.loop(0, VPG)
        def _(i):
            for xx in range(NX):
                dst = out.at[i, 0:sent[w], pl.ds(ROWS * xx, ROWS), :]
                remote(dst, dst, o_send.at[w, i, 0], o_recv.at[w, i, xx], right).wait_recv()


def body(start_block, potential):
    dma = pltpu.SemaphoreType.DMA
    any_space = pl.BlockSpec(memory_space=pl.ANY)
    field = pltpu.VMEM((VPG, GROUPS, PLANES + 4, ROWS + 16, LANES), F32)
    inner = pltpu.VMEM((VPG, GROUPS, PLANES, ROWS, LANES), F32)
    return tuple(pl.pallas_call(
        kernel,
        out_shape=(
            pltpu.VMEM(start_block.shape, F32),
            pltpu.VMEM(start_block.shape, F32),
            jax.ShapeDtypeStruct((16, 16), F32),
        ),
        in_specs=[any_space, any_space],
        out_specs=(pl.BlockSpec(memory_space=pltpu.VMEM), pl.BlockSpec(memory_space=pltpu.VMEM), pl.BlockSpec(memory_space=pltpu.VMEM)),
        scratch_shapes=[
            field, field, field, inner, inner, inner,
            pltpu.VMEM((PLANES, ROWS, LANES), F32),
            pltpu.VMEM((NX - 1, VPG, PLANES, 16, LANES), F32),
            pltpu.VMEM((NX, VPG, 2, PLANES, LANES), F32),
            pltpu.VMEM((GROUPS, VPG, 2, PLANES, LANES), F32),
            pltpu.VMEM((2, 2 * VPG, 2, 2, PLANES, LANES), F32),
            pltpu.VMEM((2, 2 * VPG, 2, 2, PLANES, LANES), F32),
            pltpu.VMEM((16, 16, 8, 128), F32),
            pltpu.VMEM((2, 8 + NZ + NY, 16, 128), F32),
            pltpu.VMEM((16, 128), F32),
            pltpu.VMEM((VPG, GROUPS, NX * ROWS, LANES), F32),
            pltpu.VMEM((VPG, NX * ROWS, LANES), F32),
            pltpu.SMEM((16, 128), F32),
            dma((VPG, 4)), dma((VPG, GROUPS)), dma((NX - 1,)), dma((NX,)), dma((GROUPS,)), dma, dma,
            dma((3, 2 * VPG, 2)), dma((3, 2 * VPG, 2)), dma((2, 2 * VPG, 2)), dma((2, 2 * VPG, 2)),
            dma((2, 8 + NZ + NY)), dma((2, 8 + NZ + NY)),
            dma((2, VPG, GROUPS)), dma((2, VPG, NX)), dma((VPG, 4)), dma((VPG, NX)), dma((VPG,)), dma((VPG,)), dma,
        ],
        compiler_params=pltpu.CompilerParams(
            collective_id=0, has_side_effects=True, vmem_limit_bytes=48 * 2**20),
        name="filtered_subspace",
    )(start_block, potential))


def solution(mesh):
    in_specs = (P("vec", "grid", None, None), P("grid", None, None))
    out_specs = (P("vec", "grid", None, None), P("vec", "grid", None, None), P())
    return jax.shard_map(body, mesh=mesh, in_specs=in_specs, out_specs=out_specs, check_vma=False)
```

```python
import functools

import jax
import jax.numpy as jnp
from jax import lax
from jax.experimental import pallas as pl
from jax.experimental.pallas import tpu as pltpu
from jax.sharding import PartitionSpec as P

MESH = pl.DeviceIdType.MESH
F32 = jnp.float32
HI = lax.Precision.HIGHEST
NX, NY, NZ = 4, 4, 8
VPG, GROUPS = 4, 4
PLANES = 4
ROWS = 48
LANES = 256
TOP, BOT = 8, 8 + ROWS
STEP = 16
AHEAD = 2
NT = (((1,), (1,)), ((), ()))


def place():
    vec, grid = lax.axis_index("vec"), lax.axis_index("grid")
    return (vec // 2) * 2 + grid % 2, grid // (2 * NZ), (grid // 2) % NZ, vec % 2


def device(x, y, z, core):
    return ((x // 2) * 2 + core, (y * NZ + z) * 2 + x % 2)


def stencil(src, pot, i, g, p, row, scale, middle):
    rows = pl.ds(row, STEP)
    at = lambda q, r: src[i, g, q, pl.ds(r, STEP), :]
    center = at(p + 2, row)
    lane = lax.broadcasted_iota(jnp.int32, (STEP, LANES), 1)
    left = jnp.where(lane == 0, 0.0, pltpu.roll(center, 1, 1))
    right = jnp.where(lane == LANES - 1, 0.0, pltpu.roll(center, LANES - 1, 1))
    cross = (at(p + 2, row - 1) + at(p + 2, row + 1)) + (left + right)
    near = at(p + 1, row) + at(p + 3, row)
    far = at(p, row) + at(p + 4, row)
    diag = scale * pot[p, pl.ds(row - TOP, STEP), :] + scale * (1.625 - middle)
    return diag * center - (scale / 3.0) * near + (scale / 48.0) * far - (scale * 0.25) * cross


def kernel(start, pot, rot_out, img_out, ritz_out,
           xs, fs, ss, aa, rr, ii, pw, edge, pack, xy, ysend, yrecv, gp, red, mat, ps, sib, inv_s,
           a_send, a_recv, e_sem, k_send, k_recv, p_send, p_recv, h_send, h_recv, y_send, y_recv,
           r_send, r_recv, o_send, o_recv, q_send, q_recv, t_send, t_recv, s_sem):
    x, y, z, c = place()
    x_lo = x % 2
    mine = lax.axis_index("vec")
    k = y * NZ + z
    ring = NY * NZ

    def at_ring(kk, core):
        kk = (kk + ring) % ring
        return device(x, kk // NZ, kk % NZ, core)

    right = at_ring(k + c, 1 - c)
    left = at_ring(k - (1 - c), 1 - c)
    line = [device(((2 * x + c + d) % 8) // 2, y, z, ((2 * x + c + d) % 8) % 2) for d in range(1, 8)]
    z_peers = [device(x, y, (z + d) % NZ, c) for d in range(1, NZ)]
    y_peers = [device(x, (y + d) % NY, z, c) for d in range(1, NY)]
    far = at_ring(k + 2 * c - 1, 1 - c)

    barrier = pltpu.get_barrier_semaphore()
    peers = line + z_peers + y_peers + [far]
    for peer in peers:
        pl.semaphore_signal(barrier, inc=1, device_id=peer, device_id_type=MESH)
    pl.semaphore_wait(barrier, len(peers))

    def remote(src, dst, send, recv, to):
        return pltpu.make_async_remote_copy(
            src_ref=src, dst_ref=dst, send_sem=send, recv_sem=recv, device_id=to, device_id_type=MESH)

    own_rows = pl.ds(TOP, ROWS)

    def pot_local():
        return pltpu.make_async_copy(pot.at[:, pl.ds(pl.multiple_of(ROWS * x, 8), ROWS), :], pw, p_recv)

    pair_x = x + 1 - 2 * x_lo
    pot_remote = remote(pot.at[:, pl.ds(pl.multiple_of(ROWS * pair_x, 8), ROWS), :], pw, p_send, p_recv,
                        device(pair_x, y, z, c))

    @pl.when(c == x_lo)
    def _():
        pot_local().start()
        pot_remote.start()

    def a_copy(i, d):
        to = (x + d) % NX
        src = start.at[i, :, pl.ds(pl.multiple_of(ROWS * to, 8), ROWS), :]
        dst = xs.at[i, mine, 2:2 + PLANES, own_rows, :]
        return src, dst, to

    def a_remote(i, d):
        src, dst, to = a_copy(i, d)
        return remote(src, dst, a_send.at[i, d], a_recv.at[i, mine], device(to, y, z, x_lo))

    def a_start(i):
        for d in (2, 1, 3):
            a_remote(i, d).start()

        @pl.when(c == x_lo)
        def _():
            src, dst, _ = a_copy(i, 0)
            pltpu.make_async_copy(src, dst, a_recv.at[i, mine]).start()

        @pl.when(c != x_lo)
        def _():
            a_remote(i, 0).start()

    def e_copy(b):
        return pltpu.make_async_copy(start.at[:, :, pl.ds(ROWS * (b + 1) - 8, 16), :], edge.at[b], e_sem.at[b])

    def k_remote(d):
        to = (x + d) % NX
        return remote(pack.at[to], xy.at[mine], k_send.at[d], k_recv.at[mine], device(to, y, z, x_lo))

    for b in range(NX - 1):
        e_copy(b).start()
    a_start(0)
    for b in range(NX - 1):
        e_copy(b).wait()

    @pl.loop(0, VPG)
    def _(i):
        for p in range(PLANES):
            for q in range(NX):
                zero = jnp.zeros((1, LANES), F32)
                above_row = edge[q - 1, i, p, pl.ds(7, 1), :] if q else zero
                below_row = edge[q, i, p, pl.ds(8, 1), :] if q < NX - 1 else zero
                pack[q, i, 0, pl.ds(p, 1), :] = above_row
                pack[q, i, 1, pl.ds(p, 1), :] = below_row

    for d in (2, 1, 3):
        k_remote(d).start()

    @pl.when(c == x_lo)
    def _():
        pltpu.make_async_copy(pack.at[x], xy.at[mine], k_recv.at[mine]).start()

    @pl.when(c != x_lo)
    def _():
        k_remote(0).start()

    @pl.loop(1, VPG)
    def _(i):
        a_start(i)

    def a_wait(n):
        i, h = n // 2, n % 2
        for e in range(2):
            dst = xs.at[i, 2 * h + e, 2:2 + PLANES, own_rows, :]
            remote(dst, dst, a_send.at[i, 0], a_recv.at[i, 2 * h + e], right).wait_recv()

    top_keep = jnp.where(x == 0, 0.0, 1.0).astype(F32)
    bot_keep = jnp.where(x == NX - 1, 0.0, 1.0).astype(F32)
    above = device((x + NX - 1) % NX, y, z, c)
    below = device((x + 1) % NX, y, z, c)

    def plane_copies(buf, s, n):
        i, gs = n // 2, pl.ds(2 * (n % 2), 2)
        return (
            remote(buf.at[i, gs, PLANES:PLANES + 2, own_rows, :], buf.at[i, gs, 0:2, own_rows, :],
                   h_send.at[s, n, 0], h_recv.at[s, n, 0], right),
            remote(buf.at[i, gs, 2:4, own_rows, :], buf.at[i, gs, PLANES + 2:PLANES + 4, own_rows, :],
                   h_send.at[s, n, 1], h_recv.at[s, n, 1], left),
        )

    def row_copies(s, n):
        return (
            remote(ysend.at[s, n, 0], yrecv.at[s, n, 0], y_send.at[s, n, 0], y_recv.at[s, n, 0], below),
            remote(ysend.at[s, n, 1], yrecv.at[s, n, 1], y_send.at[s, n, 1], y_recv.at[s, n, 1], above),
        )

    def row_start(buf, s, n):
        i, h = n // 2, n % 2
        for e in range(2):
            for p in range(PLANES):
                ysend[s, n, 0, e, pl.ds(p, 1), :] = buf[i, 2 * h + e, p + 2, pl.ds(BOT - 1, 1), :]
                ysend[s, n, 1, e, pl.ds(p, 1), :] = buf[i, 2 * h + e, p + 2, pl.ds(TOP, 1), :]

        for copy in row_copies(s, n):
            copy.start()

    def plane_start(buf, s, n):
        for copy in plane_copies(buf, s, n):
            copy.start()

    def plane_wait(buf, s, n):
        for copy in plane_copies(buf, s, n):
            copy.wait_recv()

    def row_wait(buf, s, n):
        i, h = n // 2, n % 2
        for copy in row_copies(s, n):
            copy.wait_recv()

        for e in range(2):
            for p in range(PLANES):
                buf[i, 2 * h + e, p + 2, pl.ds(TOP - 1, 1), :] = yrecv[s, n, 0, e, pl.ds(p, 1), :] * top_keep
                buf[i, 2 * h + e, p + 2, pl.ds(BOT, 1), :] = yrecv[s, n, 1, e, pl.ds(p, 1), :] * bot_keep

    def first(n):
        i = n // 2
        plane_wait(xs, 0, n)

        @pl.loop(0, 2)
        def _(e):
            g = 2 * (n % 2) + e
            for p in range(PLANES):
                xs[i, g, p + 2, pl.ds(TOP - 1, 1), :] = xy[g, i, 0, pl.ds(p, 1), :]
                xs[i, g, p + 2, pl.ds(BOT, 1), :] = xy[g, i, 1, pl.ds(p, 1), :]
            for p in range(PLANES):
                for row in range(TOP, BOT, STEP):
                    fs[i, g, p + 2, pl.ds(row, STEP), :] = stencil(xs, pw, i, g, p, row, 0.5, 3.0)

        plane_start(fs, 1, n)
        row_start(fs, 0, n)

    def block(i, gs, j, other, off):
        def step(t, accs):
            p, r = t // (ROWS // 8), t % (ROWS // 8)
            row = pl.multiple_of(TOP + 8 * r, 8)
            a = [ss[i, g, p + 2, pl.ds(row, 8), :] for g in gs]
            if off:
                b = [other[j, h, p, pl.ds(pl.multiple_of(8 * r, 8), 8), :] for h in range(GROUPS)]
            else:
                b = [other[j, h, p + 2, pl.ds(row, 8), :] for h in range(GROUPS)]
            new = []
            for q in range(len(gs)):
                for h in range(GROUPS):
                    prod = a[q] * b[h]
                    new.append(accs[q * GROUPS + h] + (prod[:, :128] + prod[:, 128:]))
            return tuple(new)

        zero = jnp.zeros((8, 128), F32)
        return lax.fori_loop(0, PLANES * ROWS // 8, step, (zero,) * (len(gs) * GROUPS))

    def blocks(n, other, off):
        i, h = n // 2, n % 2

        @pl.loop(0, i)
        def _(j):
            gs = (2 * h, 2 * h + 1)
            accs = block(i, gs, j, other, off)
            for q, g in enumerate(gs):
                for o in range(GROUPS):
                    gp[g * VPG + i, o * VPG + j] = accs[q * GROUPS + o]
                    gp[o * VPG + j, g * VPG + i] = accs[q * GROUPS + o]

        @pl.when(h == 1)
        def _():
            accs = block(i, range(GROUPS), i, other, off)
            for g in range(GROUPS):
                for o in range(GROUPS):
                    gp[g * VPG + i, o * VPG + i] = accs[g * GROUPS + o]

    def q_copy(i, j):
        to_x, to_c = 2 * (j // 2) + c, j % 2
        src = ss.at[i, :, 2 + PLANES - AHEAD + to_c, own_rows, :]
        dst = ps.at[i, :, pl.ds(pl.multiple_of(ROWS * x, 8), ROWS), :]
        here = jnp.logical_and(to_x == x, to_c == c)
        send = remote(src, dst, q_send.at[i, j], q_recv.at[i, x], device(to_x, y, z, to_c))
        return here, send, pltpu.make_async_copy(src, dst, q_recv.at[i, x])

    def q_start(i):
        for j in range(4):
            here, send, keep = q_copy(i, j)

            @pl.when(here)
            def _():
                keep.start()

            @pl.when(jnp.logical_not(here))
            def _():
                send.start()

    def second(n):
        i = n // 2
        plane_wait(fs, 1, n)
        row_wait(fs, 0, n)

        @pl.when(n == 2 * VPG - 1)
        def _():
            @pl.loop(0, VPG)
            def _(t):
                plane_start(ss, 2, t)

        @pl.loop(0, 2)
        def _(e):
            g = 2 * (n % 2) + e
            for p in range(PLANES):
                for row in range(TOP, BOT, STEP):
                    rows = pl.ds(row, STEP)
                    ss[i, g, p + 2, rows, :] = (
                        stencil(fs, pw, i, g, p, row, 1.0, 3.0) - xs[i, g, p + 2, rows, :])

        row_start(ss, 1, n)
        blocks(n, ss, False)

    def image(n):
        i = n // 2
        plane_wait(ss, 2, n)
        row_wait(ss, 1, n)

        @pl.loop(0, 2)
        def _(e):
            g = 2 * (n % 2) + e
            for p in range(PLANES):
                for row in range(TOP, BOT, STEP):
                    aa[i, g, p, pl.ds(row - TOP, STEP), :] = stencil(ss, pw, i, g, p, row, 1.0, 0.0)

        blocks(n, aa, True)

    line_slot = 2 * x + c
    lane16 = lax.broadcasted_iota(jnp.int32, (16, 128), 1)

    def gather_tiles():
        out = jnp.zeros((16, 128), F32)
        for u in range(16):
            tile = jnp.sum(gp[u], axis=1)
            out = jnp.where(lane16 == u, jnp.sum(tile, axis=1, keepdims=True), out)
        return out

    rounds = ((line, 0, 8, line_slot), (z_peers, 8, NZ, z), (y_peers, 8 + NZ, NY, y))

    def round_copies(w, n):
        to, base, count, own = rounds[n]
        slot = base + own
        return [remote(red.at[w, slot], red.at[w, slot], r_send.at[w, base + d], r_recv.at[w, slot], peer)
                for d, peer in enumerate(to)]

    def round_start(w, n, value):
        to, base, count, own = rounds[n]
        red[w, base + own] = value
        for copy in round_copies(w, n):
            copy.start()

    def round_sum(w, n):
        to, base, count, own = rounds[n]
        for d, peer in enumerate(to):
            slot = base + (own + d + 1) % count
            remote(red.at[w, slot], red.at[w, slot], r_send.at[w, base + d], r_recv.at[w, slot], peer).wait_recv()
        total = red[w, base]
        for q in range(1, count):
            total = total + red[w, base + q]
        return total

    pot_wait = remote(pw, pw, p_send, p_recv, right)

    parts = 2 * VPG

    @pl.loop(0, VPG)
    def _(i):
        for h in range(2):
            a_wait(2 * i + h)
            plane_start(xs, 0, 2 * i + h)

        @pl.when(i == 0)
        def _():
            pot_wait.wait_recv()
            for g in range(GROUPS):
                remote(xy.at[g], xy.at[g], k_send.at[0], k_recv.at[g], right).wait_recv()

        @pl.when(i < VPG - 1)
        def _():
            @pl.loop(0, 2)
            def _(h):
                first(2 * i + h)

    @pl.loop(0, parts)
    def _(t):
        @pl.when(t == parts - 4)
        def _():
            first(t + 2)

        @pl.when(t == parts - 3)
        def _():
            first(t + 2)
            q_start(1)

        second(t)

        @pl.when(t == 1)
        def _():
            q_start(0)

    round_start(0, 0, gather_tiles())
    q_start(2)
    q_start(3)
    round_start(0, 1, round_sum(0, 0))
    round_start(0, 2, round_sum(0, 1))

    gram = round_sum(0, 2)

    row16 = lax.broadcasted_iota(jnp.int32, (16, 128), 0)
    work = jnp.where(lane16 < 16, gram, jnp.where(lane16 - 16 == row16, 1.0, 0.0))
    for j in range(15):
        column = work[:, j:j + 1] * (1.0 / work[j:j + 1, j:j + 1])
        work = work - jnp.where(row16 > j, column, 0.0) * work[j:j + 1, :]
    pivots = jnp.sum(jnp.where(lane16 == row16, work, 0.0), axis=1, keepdims=True)
    work = work * (1.0 / jnp.sqrt(pivots))
    inverse = jnp.where(lane16 < 16, pltpu.roll(work, 112, 1), 0.0)
    norm = jnp.sqrt(jnp.full((16, 128), PLANES * 64 * ROWS * NX * LANES, F32))
    mat[...] = inverse * norm
    to_smem = pltpu.make_async_copy(mat, inv_s, s_sem)
    to_smem.start()
    to_smem.wait()

    sent = (PLANES - AHEAD, PLANES)

    def o_copy(out, buf, w, i, g):
        to_x = 2 * (g // 2) + c
        to_c = g % 2
        src = buf.at[i, g, 0:sent[w]]
        dst = out.at[i, 0:sent[w], pl.ds(pl.multiple_of(ROWS * x, 8), ROWS), :]
        here = jnp.logical_and(to_x == x, to_c == c)
        send = remote(src, dst, o_send.at[w, i, g], o_recv.at[w, i, x], device(to_x, y, z, to_c))
        keep = pltpu.make_async_copy(src, dst, o_recv.at[w, i, x])
        return here, send, keep

    def rotate(src, lift, buf, out, w, begin, end):
        @pl.loop(begin * GROUPS, end * GROUPS)
        def _(n):
            i, g = n // GROUPS, n % GROUPS
            v = g * VPG + i
            coef = [inv_s[v, u] for u in range(16)]

            @pl.loop(0, sent[w])
            def _(p):
                for row in range(0, ROWS, STEP):
                    acc = None
                    for u in range(16):
                        term = coef[u] * src[u % VPG, u // VPG, p + lift, pl.ds(row + (TOP if lift else 0), STEP), :]
                        acc = term if acc is None else acc + term
                    buf[i, g, p, pl.ds(row, STEP), :] = acc

            here, send, keep = o_copy(out, buf, w, i, g)

            @pl.when(here)
            def _():
                keep.start()

            @pl.when(jnp.logical_not(here))
            def _():
                send.start()

    sibling = device(x, y, z, 1 - c)
    my_plane = PLANES - AHEAD + c

    def t_copy(i):
        return remote(sib.at[i], rot_out.at[i, my_plane], t_send.at[i], t_recv.at[i], sibling)

    def rotate_ahead(core, store):
        @pl.loop(0, VPG)
        def _(i):
            v = (2 * (x // 2) + core) * VPG + i
            coef = [inv_s[v, u] for u in range(16)]

            @pl.loop(0, NX * ROWS // STEP)
            def _(r):
                rows = pl.ds(pl.multiple_of(r * STEP, STEP), STEP)
                acc = None
                for u in range(16):
                    term = coef[u] * ps[u % VPG, u // VPG, rows, :]
                    acc = term if acc is None else acc + term
                store(i, rows, acc)

    def to_sibling(i, rows, value):
        sib[i, rows, :] = value

    def to_output(i, rows, value):
        rot_out[i, my_plane, rows, :] = value

    @pl.loop(VPG, parts)
    def _(t):
        plane_start(ss, 2, t)

    rotate(ss, 2, rr, rot_out, 0, 0, VPG)

    @pl.loop(0, VPG)
    def _(i):
        for xx in range(NX):
            dst = ps.at[i, :, pl.ds(ROWS * xx, ROWS), :]
            remote(dst, dst, q_send.at[i, 0], q_recv.at[i, xx], right).wait_recv()

    rotate_ahead(1 - c, to_sibling)

    @pl.loop(0, VPG)
    def _(i):
        t_copy(i).start()

    rotate_ahead(c, to_output)

    @pl.loop(0, parts)
    def _(t):
        image(t)

    round_start(1, 1, gather_tiles())
    rotate(aa, 0, ii, img_out, 1, 0, 1)
    round_start(1, 2, round_sum(1, 1))
    rotate(aa, 0, ii, img_out, 1, 1, 2)
    round_start(1, 0, round_sum(1, 2))
    rotate(aa, 0, ii, img_out, 1, 2, VPG)
    curvature = round_sum(1, 0)
    half = lax.dot_general(inverse, curvature, NT, precision=HI, preferred_element_type=F32)
    half = jnp.concatenate([half, jnp.zeros((16, 112), F32)], axis=1)
    ritz_out[...] = lax.dot_general(half, inverse, NT, precision=HI, preferred_element_type=F32)

    @pl.when(c == x_lo)
    def _():
        pot_remote.wait_send()

    @pl.loop(0, VPG)
    def _(i):
        for d in (1, 2, 3):
            a_remote(i, d).wait_send()

        @pl.when(c != x_lo)
        def _():
            a_remote(i, 0).wait_send()

    @pl.loop(0, parts)
    def _(t):
        for s, buf in enumerate((xs, fs, ss)):
            for copy in plane_copies(buf, s, t):
                copy.wait_send()
        for s in range(2):
            for copy in row_copies(s, t):
                copy.wait_send()

    @pl.loop(0, VPG)
    def _(i):
        t_copy(i).wait_send()
        theirs = rot_out.at[i, 2 * PLANES - 2 * AHEAD + 1 - my_plane]
        remote(theirs, theirs, t_send.at[i], t_recv.at[i], sibling).wait_recv()
        for j in range(4):
            here, send, keep = q_copy(i, j)

            @pl.when(jnp.logical_not(here))
            def _():
                send.wait_send()

    for d in (1, 2, 3):
        k_remote(d).wait_send()

    @pl.when(c != x_lo)
    def _():
        k_remote(0).wait_send()

    for w in range(2):
        for n in range(3):
            for copy in round_copies(w, n):
                copy.wait_send()

    for w, (out, buf) in enumerate(((rot_out, rr), (img_out, ii))):
        @pl.loop(0, VPG * GROUPS)
        def _(n):
            i, g = n // GROUPS, n % GROUPS
            here, send, keep = o_copy(out, buf, w, i, g)

            @pl.when(jnp.logical_not(here))
            def _():
                send.wait_send()

        @pl.loop(0, VPG)
        def _(i):
            for xx in range(NX):
                dst = out.at[i, 0:sent[w], pl.ds(ROWS * xx, ROWS), :]
                remote(dst, dst, o_send.at[w, i, 0], o_recv.at[w, i, xx], right).wait_recv()


def body(start_block, potential):
    dma = pltpu.SemaphoreType.DMA
    any_space = pl.BlockSpec(memory_space=pl.ANY)
    field = pltpu.VMEM((VPG, GROUPS, PLANES + 4, ROWS + 16, LANES), F32)
    inner = pltpu.VMEM((VPG, GROUPS, PLANES, ROWS, LANES), F32)
    return tuple(pl.pallas_call(
        kernel,
        out_shape=(
            pltpu.VMEM(start_block.shape, F32),
            pltpu.VMEM(start_block.shape, F32),
            pltpu.VMEM((16, 16), F32),
        ),
        in_specs=[any_space, any_space],
        out_specs=(pl.BlockSpec(memory_space=pltpu.VMEM), pl.BlockSpec(memory_space=pltpu.VMEM), pl.BlockSpec(memory_space=pltpu.VMEM)),
        scratch_shapes=[
            field, field, field, inner, inner, inner,
            pltpu.VMEM((PLANES, ROWS, LANES), F32),
            pltpu.VMEM((NX - 1, VPG, PLANES, 16, LANES), F32),
            pltpu.VMEM((NX, VPG, 2, PLANES, LANES), F32),
            pltpu.VMEM((GROUPS, VPG, 2, PLANES, LANES), F32),
            pltpu.VMEM((2, 2 * VPG, 2, 2, PLANES, LANES), F32),
            pltpu.VMEM((2, 2 * VPG, 2, 2, PLANES, LANES), F32),
            pltpu.VMEM((16, 16, 8, 128), F32),
            pltpu.VMEM((2, 8 + NZ + NY, 16, 128), F32),
            pltpu.VMEM((16, 128), F32),
            pltpu.VMEM((VPG, GROUPS, NX * ROWS, LANES), F32),
            pltpu.VMEM((VPG, NX * ROWS, LANES), F32),
            pltpu.SMEM((16, 128), F32),
            dma((VPG, 4)), dma((VPG, GROUPS)), dma((NX - 1,)), dma((NX,)), dma((GROUPS,)), dma, dma,
            dma((3, 2 * VPG, 2)), dma((3, 2 * VPG, 2)), dma((2, 2 * VPG, 2)), dma((2, 2 * VPG, 2)),
            dma((2, 8 + NZ + NY)), dma((2, 8 + NZ + NY)),
            dma((2, VPG, GROUPS)), dma((2, VPG, NX)), dma((VPG, 4)), dma((VPG, NX)), dma((VPG,)), dma((VPG,)), dma,
        ],
        compiler_params=pltpu.CompilerParams(
            collective_id=0, has_side_effects=True, vmem_limit_bytes=48 * 2**20),
        name="filtered_subspace",
    )(start_block, potential))


def solution(mesh):
    in_specs = (P("vec", "grid", None, None), P("grid", None, None))
    out_specs = (P("vec", "grid", None, None), P("vec", "grid", None, None), P())
    return jax.shard_map(body, mesh=mesh, in_specs=in_specs, out_specs=out_specs, check_vma=False)
```

```python
import functools

import jax
import jax.numpy as jnp
from jax import lax
from jax.experimental import pallas as pl
from jax.experimental.pallas import tpu as pltpu
from jax.sharding import PartitionSpec as P

MESH = pl.DeviceIdType.MESH
F32 = jnp.float32
HI = lax.Precision.HIGHEST
NX, NY, NZ = 4, 4, 8
VPG, GROUPS = 4, 4
PLANES = 4
ROWS = 48
LANES = 256
TOP, BOT = 8, 8 + ROWS
STEP = 16
AHEAD = 2
NT = (((1,), (1,)), ((), ()))


def place():
    vec, grid = lax.axis_index("vec"), lax.axis_index("grid")
    return (vec // 2) * 2 + grid % 2, grid // (2 * NZ), (grid // 2) % NZ, vec % 2


def device(x, y, z, core):
    return ((x // 2) * 2 + core, (y * NZ + z) * 2 + x % 2)


def stencil(src, pot, i, g, p, row, scale, middle):
    rows = pl.ds(row, STEP)
    at = lambda q, r: src[i, g, q, pl.ds(r, STEP), :]
    center = at(p + 2, row)
    lane = lax.broadcasted_iota(jnp.int32, (STEP, LANES), 1)
    left = jnp.where(lane == 0, 0.0, pltpu.roll(center, 1, 1))
    right = jnp.where(lane == LANES - 1, 0.0, pltpu.roll(center, LANES - 1, 1))
    cross = (at(p + 2, row - 1) + at(p + 2, row + 1)) + (left + right)
    near = at(p + 1, row) + at(p + 3, row)
    far = at(p, row) + at(p + 4, row)
    diag = scale * pot[p, pl.ds(row - TOP, STEP), :] + scale * (1.625 - middle)
    return diag * center - (scale / 3.0) * near + (scale / 48.0) * far - (scale * 0.25) * cross


def kernel(start, pot, rot_out, img_out, ritz_out,
           xs, fs, ss, aa, rr, ii, pw, edge, pack, xy, ysend, yrecv, gp, red, mat, ps, sib, inv_s,
           a_send, a_recv, e_sem, k_send, k_recv, p_send, p_recv, h_send, h_recv, y_send, y_recv,
           r_send, r_recv, o_send, o_recv, q_send, q_recv, t_send, t_recv, s_sem):
    x, y, z, c = place()
    x_lo = x % 2
    mine = lax.axis_index("vec")
    k = y * NZ + z
    ring = NY * NZ

    def at_ring(kk, core):
        kk = (kk + ring) % ring
        return device(x, kk // NZ, kk % NZ, core)

    right = at_ring(k + c, 1 - c)
    left = at_ring(k - (1 - c), 1 - c)
    line = [device(((2 * x + c + d) % 8) // 2, y, z, ((2 * x + c + d) % 8) % 2) for d in range(1, 8)]
    z_peers = [device(x, y, (z + d) % NZ, c) for d in range(1, NZ)]
    y_peers = [device(x, (y + d) % NY, z, c) for d in range(1, NY)]
    far = at_ring(k + 2 * c - 1, 1 - c)

    barrier = pltpu.get_barrier_semaphore()
    peers = line + z_peers + y_peers + [far]
    for peer in peers:
        pl.semaphore_signal(barrier, inc=1, device_id=peer, device_id_type=MESH)
    pl.semaphore_wait(barrier, len(peers))

    def remote(src, dst, send, recv, to):
        return pltpu.make_async_remote_copy(
            src_ref=src, dst_ref=dst, send_sem=send, recv_sem=recv, device_id=to, device_id_type=MESH)

    own_rows = pl.ds(TOP, ROWS)

    def pot_local():
        return pltpu.make_async_copy(pot.at[:, pl.ds(pl.multiple_of(ROWS * x, 8), ROWS), :], pw, p_recv)

    pair_x = x + 1 - 2 * x_lo
    pot_remote = remote(pot.at[:, pl.ds(pl.multiple_of(ROWS * pair_x, 8), ROWS), :], pw, p_send, p_recv,
                        device(pair_x, y, z, c))

    @pl.when(c == x_lo)
    def _():
        pot_local().start()
        pot_remote.start()

    def a_copy(i, d):
        to = (x + d) % NX
        src = start.at[i, :, pl.ds(pl.multiple_of(ROWS * to, 8), ROWS), :]
        dst = xs.at[i, mine, 2:2 + PLANES, own_rows, :]
        return src, dst, to

    def a_remote(i, d):
        src, dst, to = a_copy(i, d)
        return remote(src, dst, a_send.at[i, d], a_recv.at[i, mine], device(to, y, z, x_lo))

    def a_start(i):
        for d in (2, 1, 3):
            a_remote(i, d).start()

        @pl.when(c == x_lo)
        def _():
            src, dst, _ = a_copy(i, 0)
            pltpu.make_async_copy(src, dst, a_recv.at[i, mine]).start()

        @pl.when(c != x_lo)
        def _():
            a_remote(i, 0).start()

    def e_copy(b):
        return pltpu.make_async_copy(start.at[:, :, pl.ds(ROWS * (b + 1) - 8, 16), :], edge.at[b], e_sem.at[b])

    def k_remote(d):
        to = (x + d) % NX
        return remote(pack.at[to], xy.at[mine], k_send.at[d], k_recv.at[mine], device(to, y, z, x_lo))

    for b in range(NX - 1):
        e_copy(b).start()
    a_start(0)
    for b in range(NX - 1):
        e_copy(b).wait()

    @pl.loop(0, VPG)
    def _(i):
        for p in range(PLANES):
            for q in range(NX):
                zero = jnp.zeros((1, LANES), F32)
                above_row = edge[q - 1, i, p, pl.ds(7, 1), :] if q else zero
                below_row = edge[q, i, p, pl.ds(8, 1), :] if q < NX - 1 else zero
                pack[q, i, 0, pl.ds(p, 1), :] = above_row
                pack[q, i, 1, pl.ds(p, 1), :] = below_row

    for d in (2, 1, 3):
        k_remote(d).start()

    @pl.when(c == x_lo)
    def _():
        pltpu.make_async_copy(pack.at[x], xy.at[mine], k_recv.at[mine]).start()

    @pl.when(c != x_lo)
    def _():
        k_remote(0).start()

    @pl.loop(1, VPG)
    def _(i):
        a_start(i)

    def a_wait(n):
        i, h = n // 2, n % 2
        for e in range(2):
            dst = xs.at[i, 2 * h + e, 2:2 + PLANES, own_rows, :]
            remote(dst, dst, a_send.at[i, 0], a_recv.at[i, 2 * h + e], right).wait_recv()

    top_keep = jnp.where(x == 0, 0.0, 1.0).astype(F32)
    bot_keep = jnp.where(x == NX - 1, 0.0, 1.0).astype(F32)
    above = device((x + NX - 1) % NX, y, z, c)
    below = device((x + 1) % NX, y, z, c)

    def plane_copies(buf, s, n):
        i, gs = n // 2, pl.ds(2 * (n % 2), 2)
        return (
            remote(buf.at[i, gs, PLANES:PLANES + 2, own_rows, :], buf.at[i, gs, 0:2, own_rows, :],
                   h_send.at[s, n, 0], h_recv.at[s, n, 0], right),
            remote(buf.at[i, gs, 2:4, own_rows, :], buf.at[i, gs, PLANES + 2:PLANES + 4, own_rows, :],
                   h_send.at[s, n, 1], h_recv.at[s, n, 1], left),
        )

    def row_copies(s, n):
        return (
            remote(ysend.at[s, n, 0], yrecv.at[s, n, 0], y_send.at[s, n, 0], y_recv.at[s, n, 0], below),
            remote(ysend.at[s, n, 1], yrecv.at[s, n, 1], y_send.at[s, n, 1], y_recv.at[s, n, 1], above),
        )

    def row_start(buf, s, n):
        i, h = n // 2, n % 2
        for e in range(2):
            for p in range(PLANES):
                ysend[s, n, 0, e, pl.ds(p, 1), :] = buf[i, 2 * h + e, p + 2, pl.ds(BOT - 1, 1), :]
                ysend[s, n, 1, e, pl.ds(p, 1), :] = buf[i, 2 * h + e, p + 2, pl.ds(TOP, 1), :]

        for copy in row_copies(s, n):
            copy.start()

    def plane_start(buf, s, n):
        for copy in plane_copies(buf, s, n):
            copy.start()

    def plane_wait(buf, s, n):
        for copy in plane_copies(buf, s, n):
            copy.wait_recv()

    def row_wait(buf, s, n):
        i, h = n // 2, n % 2
        for copy in row_copies(s, n):
            copy.wait_recv()

        for e in range(2):
            for p in range(PLANES):
                buf[i, 2 * h + e, p + 2, pl.ds(TOP - 1, 1), :] = yrecv[s, n, 0, e, pl.ds(p, 1), :] * top_keep
                buf[i, 2 * h + e, p + 2, pl.ds(BOT, 1), :] = yrecv[s, n, 1, e, pl.ds(p, 1), :] * bot_keep

    def first(n):
        i = n // 2
        plane_wait(xs, 0, n)

        @pl.loop(0, 2)
        def _(e):
            g = 2 * (n % 2) + e
            for p in range(PLANES):
                xs[i, g, p + 2, pl.ds(TOP - 1, 1), :] = xy[g, i, 0, pl.ds(p, 1), :]
                xs[i, g, p + 2, pl.ds(BOT, 1), :] = xy[g, i, 1, pl.ds(p, 1), :]
            for p in range(PLANES):
                for row in range(TOP, BOT, STEP):
                    fs[i, g, p + 2, pl.ds(row, STEP), :] = stencil(xs, pw, i, g, p, row, 0.5, 3.0)

        plane_start(fs, 1, n)
        row_start(fs, 0, n)

    def block(i, gs, j, other, off):
        def step(t, accs):
            p, r = t // (ROWS // 8), t % (ROWS // 8)
            row = pl.multiple_of(TOP + 8 * r, 8)
            a = [ss[i, g, p + 2, pl.ds(row, 8), :] for g in gs]
            if off:
                b = [other[j, h, p, pl.ds(pl.multiple_of(8 * r, 8), 8), :] for h in range(GROUPS)]
            else:
                b = [other[j, h, p + 2, pl.ds(row, 8), :] for h in range(GROUPS)]
            new = []
            for q in range(len(gs)):
                for h in range(GROUPS):
                    prod = a[q] * b[h]
                    new.append(accs[q * GROUPS + h] + (prod[:, :128] + prod[:, 128:]))
            return tuple(new)

        zero = jnp.zeros((8, 128), F32)
        return lax.fori_loop(0, PLANES * ROWS // 8, step, (zero,) * (len(gs) * GROUPS))

    def blocks(n, other, off):
        i, h = n // 2, n % 2

        @pl.loop(0, i)
        def _(j):
            gs = (2 * h, 2 * h + 1)
            accs = block(i, gs, j, other, off)
            for q, g in enumerate(gs):
                for o in range(GROUPS):
                    gp[g * VPG + i, o * VPG + j] = accs[q * GROUPS + o]
                    gp[o * VPG + j, g * VPG + i] = accs[q * GROUPS + o]

        @pl.when(h == 1)
        def _():
            accs = block(i, range(GROUPS), i, other, off)
            for g in range(GROUPS):
                for o in range(GROUPS):
                    gp[g * VPG + i, o * VPG + i] = accs[g * GROUPS + o]

    def q_copy(i, j):
        to_x, to_c = 2 * (j // 2) + c, j % 2
        src = ss.at[i, :, 2 + PLANES - AHEAD + to_c, own_rows, :]
        dst = ps.at[i, :, pl.ds(pl.multiple_of(ROWS * x, 8), ROWS), :]
        here = jnp.logical_and(to_x == x, to_c == c)
        send = remote(src, dst, q_send.at[i, j], q_recv.at[i, x], device(to_x, y, z, to_c))
        return here, send, pltpu.make_async_copy(src, dst, q_recv.at[i, x])

    def q_start(i):
        for j in range(4):
            here, send, keep = q_copy(i, j)

            @pl.when(here)
            def _():
                keep.start()

            @pl.when(jnp.logical_not(here))
            def _():
                send.start()

    def second(n):
        i = n // 2
        plane_wait(fs, 1, n)
        row_wait(fs, 0, n)

        @pl.when(n == 2 * VPG - 1)
        def _():
            @pl.loop(0, VPG)
            def _(t):
                plane_start(ss, 2, t)

        @pl.loop(0, 2)
        def _(e):
            g = 2 * (n % 2) + e
            for p in range(PLANES):
                for row in range(TOP, BOT, STEP):
                    rows = pl.ds(row, STEP)
                    ss[i, g, p + 2, rows, :] = (
                        stencil(fs, pw, i, g, p, row, 1.0, 3.0) - xs[i, g, p + 2, rows, :])

        row_start(ss, 1, n)
        blocks(n, ss, False)

    def image(n):
        i = n // 2
        plane_wait(ss, 2, n)
        row_wait(ss, 1, n)

        @pl.loop(0, 2)
        def _(e):
            g = 2 * (n % 2) + e
            for p in range(PLANES):
                for row in range(TOP, BOT, STEP):
                    aa[i, g, p, pl.ds(row - TOP, STEP), :] = stencil(ss, pw, i, g, p, row, 1.0, 0.0)

        blocks(n, aa, True)

    line_slot = 2 * x + c
    lane16 = lax.broadcasted_iota(jnp.int32, (16, 128), 1)

    def gather_tiles():
        out = jnp.zeros((16, 128), F32)
        for u in range(16):
            tile = jnp.sum(gp[u], axis=1)
            out = jnp.where(lane16 == u, jnp.sum(tile, axis=1, keepdims=True), out)
        return out

    rounds = ((line, 0, 8, line_slot), (z_peers, 8, NZ, z), (y_peers, 8 + NZ, NY, y))

    def round_copies(w, n):
        to, base, count, own = rounds[n]
        slot = base + own
        return [remote(red.at[w, slot], red.at[w, slot], r_send.at[w, base + d], r_recv.at[w, slot], peer)
                for d, peer in enumerate(to)]

    def round_start(w, n, value):
        to, base, count, own = rounds[n]
        red[w, base + own] = value
        for copy in round_copies(w, n):
            copy.start()

    def round_sum(w, n):
        to, base, count, own = rounds[n]
        for d, peer in enumerate(to):
            slot = base + (own + d + 1) % count
            remote(red.at[w, slot], red.at[w, slot], r_send.at[w, base + d], r_recv.at[w, slot], peer).wait_recv()
        total = red[w, base]
        for q in range(1, count):
            total = total + red[w, base + q]
        return total

    pot_wait = remote(pw, pw, p_send, p_recv, right)

    parts = 2 * VPG

    @pl.loop(0, VPG)
    def _(i):
        for h in range(2):
            a_wait(2 * i + h)
            plane_start(xs, 0, 2 * i + h)

        @pl.when(i == 0)
        def _():
            pot_wait.wait_recv()
            for g in range(GROUPS):
                remote(xy.at[g], xy.at[g], k_send.at[0], k_recv.at[g], right).wait_recv()

        @pl.when(i < VPG - 1)
        def _():
            @pl.loop(0, 2)
            def _(h):
                first(2 * i + h)

    @pl.loop(0, parts)
    def _(t):
        @pl.when(t == parts - 4)
        def _():
            first(t + 2)

        @pl.when(t == parts - 3)
        def _():
            first(t + 2)
            q_start(1)

        second(t)

        @pl.when(t == 1)
        def _():
            q_start(0)

    round_start(0, 0, gather_tiles())
    q_start(2)
    q_start(3)
    round_start(0, 1, round_sum(0, 0))
    round_start(0, 2, round_sum(0, 1))

    gram = round_sum(0, 2)

    row16 = lax.broadcasted_iota(jnp.int32, (16, 128), 0)
    work = jnp.where(lane16 < 16, gram, jnp.where(lane16 - 16 == row16, 1.0, 0.0))
    for j in range(15):
        column = work[:, j:j + 1] * (1.0 / work[j:j + 1, j:j + 1])
        work = work - jnp.where(row16 > j, column, 0.0) * work[j:j + 1, :]
    pivots = jnp.sum(jnp.where(lane16 == row16, work, 0.0), axis=1, keepdims=True)
    work = work * (1.0 / jnp.sqrt(pivots))
    inverse = jnp.where(lane16 < 16, pltpu.roll(work, 112, 1), 0.0)
    norm = jnp.sqrt(jnp.full((16, 128), PLANES * 64 * ROWS * NX * LANES, F32))
    mat[...] = inverse * norm
    to_smem = pltpu.make_async_copy(mat, inv_s, s_sem)
    to_smem.start()
    to_smem.wait()

    sent = (PLANES - AHEAD, PLANES)

    def o_copy(out, buf, w, i, g):
        to_x = 2 * (g // 2) + c
        to_c = g % 2
        src = buf.at[i, g, 0:sent[w]]
        dst = out.at[i, 0:sent[w], pl.ds(pl.multiple_of(ROWS * x, 8), ROWS), :]
        here = jnp.logical_and(to_x == x, to_c == c)
        send = remote(src, dst, o_send.at[w, i, g], o_recv.at[w, i, x], device(to_x, y, z, to_c))
        keep = pltpu.make_async_copy(src, dst, o_recv.at[w, i, x])
        return here, send, keep

    def rotate(src, lift, buf, out, w, begin, end):
        @pl.loop(begin * GROUPS, end * GROUPS)
        def _(n):
            i, g = n // GROUPS, n % GROUPS
            v = g * VPG + i
            coef = [inv_s[v, u] for u in range(16)]

            @pl.loop(0, sent[w])
            def _(p):
                for row in range(0, ROWS, STEP):
                    acc = None
                    for u in range(16):
                        term = coef[u] * src[u % VPG, u // VPG, p + lift, pl.ds(row + (TOP if lift else 0), STEP), :]
                        acc = term if acc is None else acc + term
                    buf[i, g, p, pl.ds(row, STEP), :] = acc

            here, send, keep = o_copy(out, buf, w, i, g)

            @pl.when(here)
            def _():
                keep.start()

            @pl.when(jnp.logical_not(here))
            def _():
                send.start()

    sibling = device(x, y, z, 1 - c)
    my_plane = PLANES - AHEAD + c

    def t_copy(i):
        return remote(sib.at[i], rot_out.at[i, my_plane], t_send.at[i], t_recv.at[i], sibling)

    def rotate_ahead(core, store):
        @pl.loop(0, VPG)
        def _(i):
            v = (2 * (x // 2) + core) * VPG + i
            coef = [inv_s[v, u] for u in range(16)]

            @pl.loop(0, NX * ROWS // STEP)
            def _(r):
                rows = pl.ds(pl.multiple_of(r * STEP, STEP), STEP)
                acc = None
                for u in range(16):
                    term = coef[u] * ps[u % VPG, u // VPG, rows, :]
                    acc = term if acc is None else acc + term
                store(i, rows, acc)

    def to_sibling(i, rows, value):
        sib[i, rows, :] = value

    def to_output(i, rows, value):
        rot_out[i, my_plane, rows, :] = value

    @pl.loop(VPG, parts)
    def _(t):
        plane_start(ss, 2, t)

    rotate(ss, 2, rr, rot_out, 0, 0, VPG)

    @pl.loop(0, parts)
    def _(t):
        image(t)

    rotate(aa, 0, ii, img_out, 1, 0, 1)
    round_start(1, 1, gather_tiles())
    @pl.loop(0, VPG)
    def _(i):
        for xx in range(NX):
            dst = ps.at[i, :, pl.ds(ROWS * xx, ROWS), :]
            remote(dst, dst, q_send.at[i, 0], q_recv.at[i, xx], right).wait_recv()

    rotate_ahead(1 - c, to_sibling)

    @pl.loop(0, VPG)
    def _(i):
        t_copy(i).start()

    rotate_ahead(c, to_output)

    round_start(1, 2, round_sum(1, 1))
    rotate(aa, 0, ii, img_out, 1, 1, 2)
    round_start(1, 0, round_sum(1, 2))
    rotate(aa, 0, ii, img_out, 1, 2, VPG)
    curvature = round_sum(1, 0)
    half = lax.dot_general(inverse, curvature, NT, precision=HI, preferred_element_type=F32)
    half = jnp.concatenate([half, jnp.zeros((16, 112), F32)], axis=1)
    ritz_out[...] = lax.dot_general(half, inverse, NT, precision=HI, preferred_element_type=F32)

    @pl.when(c == x_lo)
    def _():
        pot_remote.wait_send()

    @pl.loop(0, VPG)
    def _(i):
        for d in (1, 2, 3):
            a_remote(i, d).wait_send()

        @pl.when(c != x_lo)
        def _():
            a_remote(i, 0).wait_send()

    @pl.loop(0, parts)
    def _(t):
        for s, buf in enumerate((xs, fs, ss)):
            for copy in plane_copies(buf, s, t):
                copy.wait_send()
        for s in range(2):
            for copy in row_copies(s, t):
                copy.wait_send()

    @pl.loop(0, VPG)
    def _(i):
        t_copy(i).wait_send()
        theirs = rot_out.at[i, 2 * PLANES - 2 * AHEAD + 1 - my_plane]
        remote(theirs, theirs, t_send.at[i], t_recv.at[i], sibling).wait_recv()
        for j in range(4):
            here, send, keep = q_copy(i, j)

            @pl.when(jnp.logical_not(here))
            def _():
                send.wait_send()

    for d in (1, 2, 3):
        k_remote(d).wait_send()

    @pl.when(c != x_lo)
    def _():
        k_remote(0).wait_send()

    for w in range(2):
        for n in range(3):
            for copy in round_copies(w, n):
                copy.wait_send()

    for w, (out, buf) in enumerate(((rot_out, rr), (img_out, ii))):
        @pl.loop(0, VPG * GROUPS)
        def _(n):
            i, g = n // GROUPS, n % GROUPS
            here, send, keep = o_copy(out, buf, w, i, g)

            @pl.when(jnp.logical_not(here))
            def _():
                send.wait_send()

        @pl.loop(0, VPG)
        def _(i):
            for xx in range(NX):
                dst = out.at[i, 0:sent[w], pl.ds(ROWS * xx, ROWS), :]
                remote(dst, dst, o_send.at[w, i, 0], o_recv.at[w, i, xx], right).wait_recv()


def body(start_block, potential):
    dma = pltpu.SemaphoreType.DMA
    any_space = pl.BlockSpec(memory_space=pl.ANY)
    field = pltpu.VMEM((VPG, GROUPS, PLANES + 4, ROWS + 16, LANES), F32)
    inner = pltpu.VMEM((VPG, GROUPS, PLANES, ROWS, LANES), F32)
    return tuple(pl.pallas_call(
        kernel,
        out_shape=(
            pltpu.VMEM(start_block.shape, F32),
            pltpu.VMEM(start_block.shape, F32),
            pltpu.VMEM((16, 16), F32),
        ),
        in_specs=[any_space, any_space],
        out_specs=(pl.BlockSpec(memory_space=pltpu.VMEM), pl.BlockSpec(memory_space=pltpu.VMEM), pl.BlockSpec(memory_space=pltpu.VMEM)),
        scratch_shapes=[
            field, field, field, inner, inner, inner,
            pltpu.VMEM((PLANES, ROWS, LANES), F32),
            pltpu.VMEM((NX - 1, VPG, PLANES, 16, LANES), F32),
            pltpu.VMEM((NX, VPG, 2, PLANES, LANES), F32),
            pltpu.VMEM((GROUPS, VPG, 2, PLANES, LANES), F32),
            pltpu.VMEM((2, 2 * VPG, 2, 2, PLANES, LANES), F32),
            pltpu.VMEM((2, 2 * VPG, 2, 2, PLANES, LANES), F32),
            pltpu.VMEM((16, 16, 8, 128), F32),
            pltpu.VMEM((2, 8 + NZ + NY, 16, 128), F32),
            pltpu.VMEM((16, 128), F32),
            pltpu.VMEM((VPG, GROUPS, NX * ROWS, LANES), F32),
            pltpu.VMEM((VPG, NX * ROWS, LANES), F32),
            pltpu.SMEM((16, 128), F32),
            dma((VPG, 4)), dma((VPG, GROUPS)), dma((NX - 1,)), dma((NX,)), dma((GROUPS,)), dma, dma,
            dma((3, 2 * VPG, 2)), dma((3, 2 * VPG, 2)), dma((2, 2 * VPG, 2)), dma((2, 2 * VPG, 2)),
            dma((2, 8 + NZ + NY)), dma((2, 8 + NZ + NY)),
            dma((2, VPG, GROUPS)), dma((2, VPG, NX)), dma((VPG, 4)), dma((VPG, NX)), dma((VPG,)), dma((VPG,)), dma,
        ],
        compiler_params=pltpu.CompilerParams(
            collective_id=0, has_side_effects=True, vmem_limit_bytes=48 * 2**20),
        name="filtered_subspace",
    )(start_block, potential))


def solution(mesh):
    in_specs = (P("vec", "grid", None, None), P("grid", None, None))
    out_specs = (P("vec", "grid", None, None), P("vec", "grid", None, None), P())
    return jax.shard_map(body, mesh=mesh, in_specs=in_specs, out_specs=out_specs, check_vma=False)
```
